256 devices in a mesh: dens: 8 (over z_hi, core), sp: 32 (over y, z_lo, x).
Axes of the slice: x: 4, y: 4, z: 8 (z_hi: 4, z_lo: 2; z = z_hi * 2 + z_lo), core: 2. Of those that a mesh axis runs over, the one named last changes fastest.
Arguments:
- densities: float32 [8, 64, 512, 512], P('dens', 'sp'), may hold values from 0.2 to 5
- weights: float32 [8], P('dens'), may hold values from 0.5 to 2
- spreads: float32 [3], replicated, may hold values from 1 to 3.2, as said below
Outputs:
- barycenter: float32 [64, 512, 512], P('sp')
- scalings: float32 [8, 64, 512, 512], P('dens', 'sp')
The draws below stay inside these ranges and needn't reach their ends.
Inputs may be any that keep to these rules, and one draw needn't show every extreme that they name: The vertical width spreads[0] lies within 2.4 to 3.2 cells, the two horizontal widths within 1.0 to 2.5 cells.
All inputs are finite; a program needn't handle non-finite values.
Results may differ from the reference program's by a relative error of at most 0.0001.
Values sent between devices are 32-bit elements; how exact they have to be, the bound alone decides.
A program may use at most 64 MiB of HBM per device.

```python
import math
import jax
import jax.numpy as jnp
from jax import lax

NX = 512
NY = 512
NZ = 64
ITERS = 2
DENS = 8


def draw_spreads(key, part):
    uniform_part = jax.random.uniform(jax.random.fold_in(key, 17), (3,), jnp.float32)
    lower = jnp.array([2.4, 1.0, 1.0], jnp.float32)
    upper = jnp.array([3.2, 2.5, 2.5], jnp.float32)
    return jnp.exp(jnp.log(lower) + uniform_part * (jnp.log(upper) - jnp.log(lower)))


def level_of(key, extent, split, low, largest):
    def one(position, shards_of):
        heights = jax.random.uniform(jax.random.fold_in(jax.random.fold_in(key, 6), position), (shards_of,), jnp.float32, low / len(split), largest / len(split))
        return jnp.repeat(jnp.exp(heights), extent[position] // shards_of).reshape((-1,) + (1,) * (len(extent) - position - 1))

    factor_of = one(*split[0])
    for cut in split[1:]:
        factor_of = factor_of * one(*cut)
    return factor_of


def setup_inputs(seed: int = 0) -> dict:
    key_of = jax.random.split(jax.random.key(seed), 4)
    densities = jnp.clip(jnp.exp(math.log(5.0) - 3.218876 * jax.random.uniform(key_of[0], (DENS, NZ, NX, NY), jnp.float32) ** level_of(key_of[0], (DENS, NZ, NX, NY), ((0, 8), (1, 32)), -0.2, 0.2)), 0.2, 5.0)
    weights = jnp.clip(jnp.exp(math.log(2.0) - 1.3862944 * jax.random.uniform(key_of[1], (DENS,), jnp.float32) ** level_of(key_of[1], (DENS,), ((0, 8),), -0.2, 0.2)), 0.5, 2.0)
    spreads = draw_spreads(jax.random.fold_in(key_of[3], 71), 0)
    return {"densities": densities, "weights": weights, "spreads": spreads}


def kernel_matrix(length, spread):
    pos = jnp.arange(length).astype(jnp.float32)
    diff = (pos[:, None] - pos[None, :]) / spread
    return jnp.exp(-diff * diff) / (spread * jnp.sqrt(jnp.float32(jnp.pi)))

def convolve(field, kern_z, kern_x, kern_y):
    hp = lax.Precision.HIGHEST
    field = jnp.einsum('zxy,yk->zxk', field, kern_y, precision=hp)
    field = jnp.einsum('zxy,xk->zky', field, kern_x, precision=hp)
    return jnp.einsum('zxy,zk->kxy', field, kern_z, precision=hp)

def reference(densities, weights, spreads):
    kern_z = kernel_matrix(NZ, spreads[0])
    kern_x = kernel_matrix(NX, spreads[1])
    kern_y = kernel_matrix(NY, spreads[2])
    alpha = weights / jnp.sum(weights)

    def conv_all(stack):
        return lax.map(lambda f: convolve(f, kern_z, kern_x, kern_y), stack)
    scale_v = jnp.ones_like(densities)
    scale_w = scale_v
    barycenter = None
    for step in range(ITERS):
        scale_w = densities / conv_all(scale_v)
        marginal = scale_v * conv_all(scale_w)
        logbar = lax.optimization_barrier(jnp.sum(alpha[:, None, None, None] * jnp.log(marginal), axis=0))
        barycenter = jnp.exp(logbar)
        scale_v = scale_v * barycenter[None] / marginal
    return (barycenter, scale_w)
```

```python
import jax
import jax.numpy as jnp
from jax import lax
from jax.sharding import PartitionSpec as P


def kernel_matrix(length, spread):
    pos = jnp.arange(length).astype(jnp.float32)
    diff = (pos[:, None] - pos[None, :]) / spread
    return jnp.exp(-diff * diff) / (spread * jnp.sqrt(jnp.float32(jnp.pi)))


HI = lax.Precision.HIGHEST


def local(densities, weights, spreads):
    n_sp = lax.axis_size("sp")
    n_dens = lax.axis_size("dens")
    planes = densities.shape[1]
    nz = planes * n_sp
    nx = densities.shape[2]
    ny = densities.shape[3]
    rows = nx // n_sp
    part = rows // n_dens
    kern_z = kernel_matrix(nz, spreads[0])
    kern_x = kernel_matrix(nx, spreads[1])
    kern_y = kernel_matrix(ny, spreads[2])
    total_weight = lax.psum(weights[0], "dens")
    own_weight = weights[0]
    target = densities[0]

    def to_columns(field):
        return lax.all_to_all(field, "sp", split_axis=1, concat_axis=0, tiled=True)

    def to_planes(field):
        return lax.all_to_all(field, "sp", split_axis=0, concat_axis=1, tiled=True)

    def forward(field):
        field = jnp.einsum("zxy,yk->zxk", field, kern_y, precision=HI)
        field = jnp.einsum("zxy,xk->zky", field, kern_x, precision=HI)
        return jnp.einsum("zxy,zk->kxy", to_columns(field), kern_z, precision=HI)

    def backward(field):
        field = jnp.einsum("zxy,zk->kxy", field, kern_z, precision=HI)
        field = to_planes(field)
        field = jnp.einsum("zxy,xk->zky", field, kern_x, precision=HI)
        return jnp.einsum("zxy,yk->zxk", field, kern_y, precision=HI)

    sum_z = jnp.sum(kern_z, axis=0)
    own_z = lax.dynamic_slice_in_dim(sum_z, lax.axis_index("sp") * planes, planes)
    ones = (
        own_z[:, None, None]
        * jnp.sum(kern_x, axis=0)[None, :, None]
        * jnp.sum(kern_y, axis=0)[None, None, :]
    )
    marginal = forward(target / ones)
    summed = lax.psum(own_weight * jnp.log(marginal), "dens")
    scale_v = jnp.exp(summed / total_weight) / marginal
    scale_w = target / backward(scale_v)
    marginal = scale_v * forward(scale_w)
    term = own_weight * jnp.log(marginal)
    share = lax.psum_scatter(term, "dens", scatter_dimension=1, tiled=True)
    share = jnp.exp(share / total_weight)
    share = lax.all_to_all(
        share.reshape(n_sp, planes, part, ny), "sp", split_axis=0, concat_axis=0, tiled=True
    )
    whole = lax.all_gather(share, "dens")
    barycenter = whole.transpose(2, 1, 0, 3, 4).reshape(planes, nx, ny)
    return (barycenter, scale_w[None])


def solution(mesh):
    return jax.shard_map(
        local,
        mesh=mesh,
        in_specs=(P("dens", "sp", None, None), P("dens"), P()),
        out_specs=(P("sp", None, None), P("dens", "sp", None, None)),
        check_vma=False,
    )
```

```python
import functools
import math

import jax
import jax.numpy as jnp
from jax import lax
from jax.experimental import pallas as pl
from jax.experimental.pallas import tpu as pltpu
from jax.sharding import PartitionSpec as P

MESH = pl.DeviceIdType.MESH
BF = jnp.bfloat16
F32 = jnp.float32

NXD, NYD, NZD, NHD = 4, 4, 2, 4
CH = 4
SIZE = {"x": NXD, "y": NYD, "z": NZD}
AXES = (("z", "x", "y"), ("z", "x", "y"), ("z", "x", "y"))


def order():
    steps = []
    steps += [("conv", 0, 0), ("conv", 0, 1)]
    flow = [("adv", 0, 0), ("adv", 0, 1), ("zf", 0), ("cs", 0), ("rs1", 0), ("rs2", 0), ("ag1", 0), ("ag2", 0), ("zb", 0), ("adv", 1, 0), ("adv", 1, 1)]
    when = [6.5, 13, 20, 22.5, 26, 30.5, 35, 38.5, 41, 47, 53.5]
    lag = [5, 5, 4, 4, 4.5, 5, 5.5, 5.5, 5.5, 5.5, 5.5]
    timed = []
    for c in range(CH):
        for i, step in enumerate(flow):
            timed.append((when[i] + c * lag[i], i, step + (c,)))
    steps += [t[2] for t in sorted(timed)]
    steps += [("xb", 0), ("xb", 1), ("yb",)]
    steps += [("conv", 2, 0), ("conv", 2, 1)]
    flow = [("adv", 2, 0), ("adv", 2, 1), ("zf", 2), ("cs", 2), ("rs1", 2), ("rs2", 2)]
    timed = []
    for c in range(CH):
        for i, step in enumerate(flow):
            timed.append((when[i] + c * lag[i], i, step + (c,)))
    steps += [t[2] for t in sorted(timed)]
    steps += [("tail",)]
    return steps


def split(x):
    hi = x.astype(BF)
    return hi, (x - hi.astype(F32)).astype(BF)


def dot(a, b):
    return jnp.dot(a, b, preferred_element_type=F32)


def body(
    dens_ref, wt_ref, spread_ref, bary_ref, w_ref,
    b0, b1, b2, d_ref, t_ref, cb_ref, u_ref, r1_ref, r2_ref, bar_ref, oth_ref,
    share_ref, gath_ref, whi, wlo, thi, tlo, gxh, gxl, gyh, gyl, gz3, wts, send_sem, recv_sem,
):
    dens = lax.axis_index("dens")
    sp = lax.axis_index("sp")
    zh, core = dens // 2, lax.rem(dens, 2)
    me = {"y": sp // 8, "z": lax.rem(sp // 4, 2), "x": lax.rem(sp, 4)}

    def device(h=zh, k=core, **at):
        at = {**me, **at}
        return {"dens": h * 2 + k, "sp": (at["y"] * 2 + at["z"]) * 4 + at["x"]}

    def around(axis, k):
        return lax.rem(me[axis] + k, SIZE[axis])

    right, left = lax.rem(zh + 1, 4), lax.rem(zh + 3, 4)
    far = lax.rem(zh + 2, 4)
    peers = [device(**{axis: around(axis, k)}) for axis in "xyz" for k in range(1, SIZE[axis])]
    peers += [device(k=1 - core), device(h=right), device(h=left), device(h=far)]

    barrier = pltpu.get_barrier_semaphore()
    for peer in peers:
        pl.semaphore_signal(barrier, 1, device_id=peer, device_id_type=MESH)

    root = math.sqrt(math.pi)

    def gauss(i, j, s):
        diff = (i.astype(F32) - j.astype(F32)) / s
        return jnp.exp(-diff * diff) / (s * jnp.float32(root))

    def wide(hi_ref, lo_ref, s):
        def tile(m, carry):
            at = pl.multiple_of(m * 128, 128)
            i = lax.broadcasted_iota(jnp.int32, (128, 512), 0) + at
            j = lax.broadcasted_iota(jnp.int32, (128, 512), 1)
            hi, lo = split(gauss(i, j, s))
            hi_ref[pl.ds(at, 128), :] = hi
            lo_ref[pl.ds(at, 128), :] = lo
            return carry
        lax.fori_loop(0, 4, tile, 0)

    wide(gxh, gxl, spread_ref[1])
    wide(gyh, gyl, spread_ref[2])

    def plane(q):
        return ((q >> 3) & 3) * 16 + ((q >> 2) & 1) * 8 + (q & 3) * 2 + (q >> 5)

    i = lax.broadcasted_iota(jnp.int32, (64, 192), 0)
    j = lax.broadcasted_iota(jnp.int32, (64, 192), 1)
    hi, lo = split(gauss(plane(i), plane(j & 63), spread_ref[0]))
    gz3[...] = jnp.where(j < 128, hi.astype(F32), lo.astype(F32)).astype(BF)

    def line(n, s, at, axis):
        shape = (at.shape[0], n) if axis == 1 else (n, at.shape[1])
        other = lax.broadcasted_iota(jnp.int32, shape, axis)
        return jnp.sum(gauss(at, other, s), axis=axis, keepdims=True)

    sum_y = line(512, spread_ref[2], lax.broadcasted_iota(jnp.int32, (1, 512), 1), 0)
    planes = sp * 2 + lax.broadcasted_iota(jnp.int32, (8, 1), 0)
    sum_z = line(64, spread_ref[0], planes, 1)

    for p in range(2):
        def first(m, carry):
            at = pl.multiple_of(m * 128, 128)
            rows = pl.ds(pl.multiple_of(p * 512 + m * 128, 128), 128)
            sum_x = line(512, spread_ref[1], lax.broadcasted_iota(jnp.int32, (128, 1), 0) + at, 1)
            ones = (sum_x * sum_z[p : p + 1, :]) * sum_y
            hi, lo = split(dens_ref[rows, :] / ones)
            whi[rows, :] = hi
            wlo[rows, :] = lo
            return carry
        lax.fori_loop(0, 4, first, 0)

    pl.semaphore_wait(barrier, len(peers))

    sent = []
    count = [0]

    def remote(src, dst, to):
        n = count[0]
        count[0] += 1
        copy = pltpu.make_async_remote_copy(
            src, dst, send_sem.at[n], recv_sem.at[n], device_id=to, device_id_type=MESH
        )
        copy.start()
        sent.append(copy)
        return copy.wait_recv

    def local(src, dst):
        n = count[0]
        count[0] += 1
        copy = pltpu.make_async_copy(src, dst, recv_sem.at[n])
        copy.start()
        return copy.wait

    pending = {}

    def finish(*key):
        for wait in pending.pop(key):
            wait()

    def slot(ref, lead, axis, k):
        tail = {"y": (slice(None), k), "z": (slice(None), slice(None), k), "x": (slice(None), slice(None), slice(None), k)}
        return ref.at[lead + tail[axis]]

    def swap(src, s_lead, dst, d_lead, axis):
        waits = []
        own = me[axis]
        for k in range(1, SIZE[axis]):
            to = around(axis, k)
            waits.append(remote(slot(src, s_lead, axis, to), slot(dst, d_lead, axis, own), device(**{axis: to})))
        waits.append(local(slot(src, s_lead, axis, own), slot(dst, d_lead, axis, own)))
        return waits

    bufs = (b0, b1, b2)

    def start(a, j, c):
        pending["a2a", a, j, c] = swap(bufs[a], (j, c), bufs[a], (j + 1, c), AXES[a][j])

    wts[0] = jnp.full((8, 128), wt_ref[0], F32)
    pending["wc",] = [remote(wts.at[0], wts.at[1], device(k=1 - core))]

    def weights():
        finish("wc")
        wts[2] = wts[0] + wts[1]
        pending["wh",] = [
            remote(wts.at[2], wts.at[2 + k], device(h=lax.rem(zh + k, 4))) for k in range(1, 4)
        ]

    def total_weight():
        finish("wh")
        wts[6] = 1.0 / (wts[2] + wts[3] + (wts[4] + wts[5]))

    def step_adv(a, j, c):
        finish("a2a", a, j, c)
        start(a, j + 1, c)

    def step_conv(a, h):
        cols = slice(h * 256, h * 256 + 256)

        def along_y(m, carry):
            rows = pl.ds(pl.multiple_of(m * 256, 256), 256)
            x = dot(whi[rows, :], gyh[:, cols]) + (dot(wlo[rows, :], gyh[:, cols]) + dot(whi[rows, :], gyl[:, cols]))
            hi, lo = split(x)
            thi[rows, :] = hi
            tlo[rows, :] = lo
            return carry
        lax.fori_loop(0, 4, along_y, 0)

        for p in range(2):
            def along_x(m, carry):
                rows = pl.ds(pl.multiple_of(m * 128, 128), 128)
                k = slice(p * 512, p * 512 + 512)
                x = dot(gxh[rows, :], thi[k, :]) + (dot(gxl[rows, :], thi[k, :]) + dot(gxh[rows, :], tlo[k, :]))
                for e in range(2):
                    bufs[a][0, 2 * h + e, p, m] = x[:, e * 128 : e * 128 + 128].reshape(2, 4, 16, 128)
                return carry
            lax.fori_loop(0, 4, along_x, 0)
        for e in range(2):
            start(a, 0, 2 * h + e)
        if a == 0 and h == 1:
            weights()

    def columns(x):
        hi, lo = split(x)
        return dot(gz3[...], jnp.concatenate([hi, lo, hi], axis=0))

    own_rows = pl.ds(core * 8, 8)
    other_rows = pl.ds((1 - core) * 8, 8)

    def step_zf(a, c):
        finish("a2a", a, 2, c)
        flat = bufs[a].at[3, c].reshape(1024, 128)
        ph = a // 2
        weight = wt_ref[0]

        def pair(n, carry):
            r = n * 2
            x = jnp.concatenate([flat[pl.ds(r + e, 64, stride=16), :] for e in range(2)], axis=1)
            y = columns(x)
            for e in range(2):
                part = y[:, e * 128 : e * 128 + 128]
                if a == 0:
                    d_ref[c, r + e] = part
                else:
                    part = d_ref[c, r + e] * part
                t_ref[ph, c, r + e] = weight * jnp.log(part)
            return carry
        lax.fori_loop(0, 8, pair, 0)
        pending["cs", ph, c] = [remote(t_ref.at[ph, c, other_rows], cb_ref.at[ph, c], device(k=1 - core))]

    def rows_of(h, n=2, off=0):
        return pl.ds(h * 2 + off, n)

    def step_cs(a, c):
        ph = a // 2
        finish("cs", ph, c)
        u_ref[ph, c] = t_ref[ph, c, own_rows] + cb_ref[ph, c]
        pending["rs1", ph, c] = [
            remote(u_ref.at[ph, c, rows_of(far, 1, 0)], r1_ref.at[ph, c, 0], device(h=right)),
            remote(u_ref.at[ph, c, rows_of(far, 1, 1)], r1_ref.at[ph, c, 1], device(h=left)),
        ]

    def step_rs1(a, c):
        ph = a // 2
        finish("rs1", ph, c)
        u_ref[ph, c, rows_of(right, 1, 0)] += r1_ref[ph, c, 0]
        u_ref[ph, c, rows_of(left, 1, 1)] += r1_ref[ph, c, 1]
        pending["rs2", ph, c] = [
            remote(u_ref.at[ph, c, rows_of(right)], r2_ref.at[ph, c, 0], device(h=right)),
            remote(u_ref.at[ph, c, rows_of(left)], r2_ref.at[ph, c, 1], device(h=left)),
        ]

    def step_rs2(a, c):
        ph = a // 2
        if a == 0 and c == 0:
            total_weight()
        finish("rs2", ph, c)
        total = u_ref[ph, c, rows_of(zh)] + (r2_ref[ph, c, 0] + r2_ref[ph, c, 1])
        mean = jnp.exp(total * wts[6, 0:1, 0:1].reshape(1, 1, 1))
        if a == 0:
            bar_ref[c, rows_of(zh)] = mean
            here = bar_ref.at[c, rows_of(zh)]
            pending["ag1", c] = [remote(here, here, device(h=right)), remote(here, here, device(h=left))]
        else:
            flat = share_ref.at[0].reshape(512, 128)
            for e in range(2):
                flat[pl.ds(c * 2 + e, 64, stride=8), :] = mean[e]

    def step_ag1(a, c):
        finish("ag1", c)
        one = bar_ref.at[c, rows_of(left, 1, 0)]
        two = bar_ref.at[c, rows_of(right, 1, 1)]
        pending["ag2", c] = [remote(one, one, device(h=right)), remote(two, two, device(h=left))]

    def step_ag2(a, c):
        finish("ag2", c)
        pending["cg", c] = [remote(bar_ref.at[c], oth_ref.at[c], device(k=1 - core))]

    def step_zb(a, c):
        flat = b1.at[0, c].reshape(1024, 128)

        def half(src, first):
            def pair(n, carry):
                r = first + n * 2
                parts = []
                for e in range(2):
                    v = src[c, n * 2 + e] / d_ref[c, r + e]
                    d_ref[c, r + e] = v
                    parts.append(v)
                y = columns(jnp.concatenate(parts, axis=1))
                for e in range(2):
                    flat[pl.ds(r + e, 64, stride=16), :] = y[:, e * 128 : e * 128 + 128]
                return carry
            lax.fori_loop(0, 4, pair, 0)

        half(bar_ref, core * 8)
        finish("cg", c)
        half(oth_ref, (1 - core) * 8)
        start(1, 0, c)

    def step_xb(h):
        for e in range(2):
            finish("a2a", 1, 2, 2 * h + e)
        cols = slice(h * 256, h * 256 + 256)
        for p in range(2):
            x = jnp.concatenate([b1[3, 2 * h + e, p].reshape(512, 128) for e in range(2)], axis=1)
            hi, lo = split(x)
            thi[p * 512 : p * 512 + 512, :] = hi
            tlo[p * 512 : p * 512 + 512, :] = lo

            def along_x(m, carry):
                rows = pl.ds(pl.multiple_of(m * 128, 128), 128)
                to = pl.ds(pl.multiple_of(p * 512 + m * 128, 128), 128)
                k = slice(p * 512, p * 512 + 512)
                x = dot(gxh[rows, :], thi[k, :]) + (dot(gxl[rows, :], thi[k, :]) + dot(gxh[rows, :], tlo[k, :]))
                hi, lo = split(x)
                whi[to, cols] = hi
                wlo[to, cols] = lo
                return carry
            lax.fori_loop(0, 4, along_x, 0)

    def step_yb():
        def along_y(m, carry):
            rows = pl.ds(pl.multiple_of(m * 128, 128), 128)
            a_hi, a_lo = whi[rows, :], wlo[rows, :]
            x = dot(a_hi, gyh[...]) + (dot(a_lo, gyh[...]) + dot(a_hi, gyl[...]))
            w = dens_ref[rows, :] / x
            w_ref[rows, :] = w
            hi, lo = split(w)
            whi[rows, :] = hi
            wlo[rows, :] = lo
            return carry
        lax.fori_loop(0, 8, along_y, 0)

    def step_tail():
        for wait in swap(share_ref, (0,), share_ref, (1,), "x"):
            wait()
        for wait in swap(share_ref, (1,), share_ref, (2,), "y"):
            wait()
        for wait in swap(share_ref, (2,), gath_ref, (core, zh), "z"):
            wait()

        def across(*at):
            here = gath_ref.at[(core,) + at]
            return remote(here, here, device(k=1 - core))

        here = gath_ref.at[core, zh]
        ring = [remote(here, here, device(h=right)), remote(here, here, device(h=left))]
        over = [across(zh)]
        for wait in ring:
            wait()
        one, two = gath_ref.at[core, left, 0], gath_ref.at[core, right, 1]
        ring = [remote(one, one, device(h=right)), remote(two, two, device(h=left))]
        over += [across(left), across(right)]
        for wait in ring:
            wait()
        over += [across(far)]
        for wait in over:
            wait()

        def place(n, carry):
            src = gath_ref.at[n >> 2, n & 3].reshape(512, 128)
            for c in range(CH):
                for e in range(2):
                    dst = bary_ref.at[c]
                    dst[pl.ds(n * 2 + e, 64, stride=16), :] = src[pl.ds(c * 2 + e, 64, stride=8), :]
            return carry
        lax.fori_loop(0, 8, place, 0)

    table = {
        "conv": step_conv, "adv": step_adv, "zf": step_zf, "cs": step_cs, "rs1": step_rs1, "rs2": step_rs2,
        "ag1": step_ag1, "ag2": step_ag2, "zb": step_zb, "xb": step_xb, "yb": step_yb, "tail": step_tail,
    }
    for name, *rest in order():
        table[name](*rest)
    for copy in sent:
        copy.wait_send()
    assert count[0] <= SEMS and not pending


SEMS = 240


def local(densities, weights, spreads):
    field = (4, CH, 2, 4, 2, 4, 16, 128)
    vmem = pltpu.VMEM
    scratch = [
        vmem(field, F32), vmem(field, F32), vmem(field, F32),
        vmem((CH, 16, 64, 128), F32),
        vmem((2, CH, 16, 64, 128), F32),
        vmem((2, CH, 8, 64, 128), F32),
        vmem((2, CH, 8, 64, 128), F32),
        vmem((2, CH, 2, 1, 64, 128), F32),
        vmem((2, CH, 2, 2, 64, 128), F32),
        vmem((CH, 8, 64, 128), F32),
        vmem((CH, 8, 64, 128), F32),
        vmem((3, 2, 4, 2, 4, 8, 128), F32),
        vmem((2, 4, 2, 4, 2, 4, 8, 128), F32),
        vmem((1024, 512), BF), vmem((1024, 512), BF),
        vmem((1024, 256), BF), vmem((1024, 256), BF),
        vmem((512, 512), BF), vmem((512, 512), BF), vmem((512, 512), BF), vmem((512, 512), BF),
        vmem((64, 192), BF),
        vmem((7, 8, 128), F32),
        pltpu.SemaphoreType.DMA((SEMS,)), pltpu.SemaphoreType.DMA((SEMS,)),
    ]
    whole = pl.BlockSpec(memory_space=pltpu.VMEM)
    smem = pl.BlockSpec(memory_space=pltpu.SMEM)
    bary, scale_w = pl.pallas_call(
        body,
        out_shape=[
            jax.ShapeDtypeStruct((CH, 1024, 128), F32),
            jax.ShapeDtypeStruct((1024, 512), F32),
        ],
        in_specs=[whole, smem, smem],
        out_specs=[whole, whole],
        scratch_shapes=scratch,
        compiler_params=pltpu.CompilerParams(
            collective_id=0, has_side_effects=True, vmem_limit_bytes=61 * 1024 * 1024
        ),
        name="sinkhorn",
    )(densities.reshape(1024, 512), weights, spreads)
    bary = bary.reshape(CH, 2, 512, 128).transpose(1, 2, 0, 3).reshape(2, 512, 512)
    return bary, scale_w.reshape(1, 2, 512, 512)


def solution(mesh):
    return jax.shard_map(
        local,
        mesh=mesh,
        in_specs=(P("dens", "sp", None, None), P("dens"), P()),
        out_specs=(P("sp", None, None), P("dens", "sp", None, None)),
        check_vma=False,
    )
```

```python
import functools
import math

import jax
import jax.numpy as jnp
from jax import lax
from jax.experimental import pallas as pl
from jax.experimental.pallas import tpu as pltpu
from jax.sharding import PartitionSpec as P

MESH = pl.DeviceIdType.MESH
BF = jnp.bfloat16
F32 = jnp.float32

NXD, NYD, NZD, NHD = 4, 4, 2, 4
CH = 4
SIZE = {"x": NXD, "y": NYD, "z": NZD}
AXES = (
    ("zxy", "xyz", "zxy", "zyx"),
    ("xyz", "xyz", "xyz", "zxy"),
    ("xyz", "zxy", "yxz", "zxy"),
)


ORDER = (
    ("conv", 0, 0), ("conv", 0, 1), ("adv", 0, 0, 0), ("adv", 0, 0, 1), ("adv", 0, 0, 2), ("adv", 0, 1, 0), ("adv", 0, 1, 1),
    ("adv", 0, 0, 3), ("adv", 0, 1, 2), ("zf", 0, 0), ("zf", 0, 1), ("cs", 0, 0), ("cs", 0, 1), ("adv", 0, 1, 3), ("rs1", 0, 0),
    ("rs1", 0, 1), ("zf", 0, 2), ("rs2", 0, 0), ("zf", 0, 3), ("cs", 0, 2), ("rs2", 0, 1), ("cs", 0, 3), ("ag1", 0, 0),
    ("rs1", 0, 2), ("ag1", 0, 1), ("rs1", 0, 3), ("ag2", 0, 0), ("rs2", 0, 2), ("zb", 0, 0), ("ag2", 0, 1), ("rs2", 0, 3),
    ("zb", 0, 1), ("ag1", 0, 2), ("ag1", 0, 3), ("adv", 1, 0, 0), ("ag2", 0, 2), ("ag2", 0, 3), ("zb", 0, 2), ("adv", 1, 0, 1),
    ("zb", 0, 3), ("adv", 1, 1, 0), ("adv", 1, 0, 2), ("adv", 1, 1, 1), ("adv", 1, 0, 3), ("adv", 1, 1, 2), ("adv", 1, 1, 3),
    ("xb", 0), ("xb", 1), ("yb",), ("conv", 2, 0), ("conv", 2, 1), ("adv", 2, 0, 0), ("adv", 2, 0, 1), ("adv", 2, 0, 2),
    ("adv", 2, 0, 3), ("adv", 2, 1, 0), ("adv", 2, 1, 1), ("adv", 2, 1, 2), ("zf", 2, 0), ("zf", 2, 1), ("adv", 2, 1, 3),
    ("cs", 2, 0), ("cs", 2, 1), ("zf", 2, 2), ("rs1", 2, 0), ("rs1", 2, 1), ("cs", 2, 2), ("zf", 2, 3), ("rs2", 2, 0),
    ("cs", 2, 3), ("rs2", 2, 1), ("tx", 0), ("rs1", 2, 2), ("rs1", 2, 3), ("ty", 0), ("rs2", 2, 2), ("tz", 0), ("rs2", 2, 3),
    ("tx", 1), ("tg", 0), ("ty", 1), ("tz", 1), ("th", 0), ("tg", 1), ("ti", 0), ("tp", 0), ("th", 1), ("ti", 1), ("tp", 1),
)


def split(x):
    hi = x.astype(BF)
    return hi, (x - hi.astype(F32)).astype(BF)


def dot(a, b):
    return jnp.dot(a, b, preferred_element_type=F32)


def body(
    dens_hbm, wt_ref, spread_ref, bary_hbm, w_hbm,
    dens_ref, w_ref, bary_ref, inv_x, b0, b1, b2, d_ref, t_ref, cb_ref, u_ref, r1_ref, r2_ref, bar_ref, oth_ref,
    share_ref, gath_ref, whi, wlo, thi, tlo, gxh, gxl, gyh, gyl, gz3, wts, io_sem, send_sem, recv_sem,
):
    dens = lax.axis_index("dens")
    sp = lax.axis_index("sp")
    zh, core = dens // 2, lax.rem(dens, 2)
    me = {"y": sp // 8, "z": lax.rem(sp // 4, 2), "x": lax.rem(sp, 4)}

    def device(h=zh, k=core, **at):
        at = {**me, **at}
        return {"dens": h * 2 + k, "sp": (at["y"] * 2 + at["z"]) * 4 + at["x"]}

    def around(axis, k):
        return lax.rem(me[axis] + k, SIZE[axis])

    right, left = lax.rem(zh + 1, 4), lax.rem(zh + 3, 4)
    far = lax.rem(zh + 2, 4)
    peers = [device(**{axis: around(axis, k)}) for axis in "xyz" for k in range(1, SIZE[axis])]
    peers += [device(k=1 - core), device(h=right), device(h=left), device(h=far)]

    barrier = pltpu.get_barrier_semaphore()
    for peer in peers:
        pl.semaphore_signal(barrier, 1, device_id=peer, device_id_type=MESH)

    fetch = pltpu.make_async_copy(dens_hbm, dens_ref, io_sem.at[0])
    fetch.start()
    root = math.sqrt(math.pi)

    def gauss(i, j, s):
        diff = (i - j).astype(F32) * (1.0 / s)
        return jnp.exp(-diff * diff) * (1.0 / (s * jnp.float32(root)))

    def wide(hi_ref, lo_ref, s):
        def tile(m, total):
            at = pl.multiple_of(m * 64, 64)
            i = lax.broadcasted_iota(jnp.int32, (64, 512), 0) + at
            j = lax.broadcasted_iota(jnp.int32, (64, 512), 1)
            g = gauss(i, j, s)
            hi, lo = split(g)
            hi_ref[pl.ds(at, 64), :] = hi
            lo_ref[pl.ds(at, 64), :] = lo
            if hi_ref is gxh:
                inv_x[pl.ds(at, 64), :] = jnp.broadcast_to(1.0 / jnp.sum(g, axis=1, keepdims=True), (64, 128))
                return total
            return total + jnp.sum(g, axis=0, keepdims=True)
        return lax.fori_loop(0, 8, tile, jnp.zeros((1, 512), F32))

    sum_y = wide(gyh, gyl, spread_ref[2])
    wide(gxh, gxl, spread_ref[1])

    def plane(q):
        return ((q >> 3) & 3) * 16 + ((q >> 2) & 1) * 8 + (q & 3) * 2 + (q >> 5)

    i = lax.broadcasted_iota(jnp.int32, (64, 192), 0)
    j = lax.broadcasted_iota(jnp.int32, (64, 192), 1)
    hi, lo = split(gauss(plane(i), plane(j & 63), spread_ref[0]))
    gz3[...] = jnp.where(j < 128, hi.astype(F32), lo.astype(F32)).astype(BF)

    planes = sp * 2 + lax.broadcasted_iota(jnp.int32, (8, 128), 0)
    others = lax.broadcasted_iota(jnp.int32, (8, 128), 1)
    near = jnp.where(others < 64, gauss(planes, others, spread_ref[0]), 0.0)
    sum_z = jnp.sum(near, axis=1, keepdims=True)

    fetch.wait()
    for p in range(2):
        inv_y = 1.0 / (sum_y * sum_z[p : p + 1, :])

        def first(m, carry):
            rows = pl.ds(pl.multiple_of(p * 512 + m * 64, 64), 64)
            inv = inv_x[pl.ds(pl.multiple_of(m * 64, 64), 64), :]
            hi, lo = split(dens_ref[rows, :] * jnp.concatenate([inv] * 4, axis=1) * inv_y)
            whi[rows, :] = hi
            wlo[rows, :] = lo
            return carry
        lax.fori_loop(0, 8, first, 0)

    pl.semaphore_wait(barrier, len(peers))

    sent = []
    outs = []
    count = [0]

    def remote(src, dst, to):
        n = count[0]
        count[0] += 1
        copy = pltpu.make_async_remote_copy(
            src, dst, send_sem.at[n], recv_sem.at[n], device_id=to, device_id_type=MESH
        )
        copy.start()
        sent.append(copy)
        return copy.wait_recv

    def local(src, dst):
        n = count[0]
        count[0] += 1
        copy = pltpu.make_async_copy(src, dst, recv_sem.at[n])
        copy.start()
        return copy.wait

    pending = {}

    def finish(*key):
        for wait in pending.pop(key):
            wait()

    def slot(ref, lead, axis, k):
        tail = {"y": (slice(None), k), "z": (slice(None), slice(None), k), "x": (slice(None), slice(None), slice(None), k)}
        return ref.at[lead + tail[axis]]

    def swap(src, s_lead, dst, d_lead, axis, h=None):
        waits = []
        own = me[axis]

        def piece(ref, lead, k):
            ref = slot(ref, lead, axis, k)
            return ref if h is None else part(ref, h)

        for k in range(1, SIZE[axis]):
            to = around(axis, k)
            waits.append(remote(piece(src, s_lead, to), piece(dst, d_lead, own), device(**{axis: to})))
        waits.append(local(piece(src, s_lead, own), piece(dst, d_lead, own)))
        return waits

    bufs = (b0, b1, b2)

    def start(a, j, c):
        pending["a2a", a, j, c] = swap(bufs[a], (j, c), bufs[a], (j + 1, c), AXES[a][c][j])

    wts[0] = jnp.full((8, 128), wt_ref[0], F32)
    pending["wc",] = [remote(wts.at[0], wts.at[1], device(k=1 - core))]

    def weights():
        finish("wc")
        wts[2] = wts[0] + wts[1]
        pending["wh",] = [
            remote(wts.at[2], wts.at[2 + k], device(h=lax.rem(zh + k, 4))) for k in range(1, 4)
        ]

    def total_weight():
        finish("wh")
        wts[6] = 1.0 / (wts[2] + wts[3] + (wts[4] + wts[5]))

    def step_adv(a, j, c):
        finish("a2a", a, j, c)
        start(a, j + 1, c)

    def step_conv(a, h):
        cols = slice(h * 256, h * 256 + 256)

        def along_y(m, carry):
            rows = pl.ds(pl.multiple_of(m * 256, 256), 256)
            x = dot(whi[rows, :], gyh[:, cols]) + (dot(wlo[rows, :], gyh[:, cols]) + dot(whi[rows, :], gyl[:, cols]))
            hi, lo = split(x)
            thi[rows, :] = hi
            tlo[rows, :] = lo
            return carry
        lax.fori_loop(0, 4, along_y, 0)

        for p in range(2):
            def along_x(m, carry):
                rows = pl.ds(pl.multiple_of(m * 128, 128), 128)
                k = slice(p * 512, p * 512 + 512)
                x = dot(gxh[rows, :], thi[k, :]) + (dot(gxl[rows, :], thi[k, :]) + dot(gxh[rows, :], tlo[k, :]))
                for e in range(2):
                    bufs[a][0, 2 * h + e, p, m] = x[:, e * 128 : e * 128 + 128].reshape(2, 4, 16, 128)
                return carry
            lax.fori_loop(0, 4, along_x, 0)
        for e in range(2):
            start(a, 0, 2 * h + e)
        if a == 0 and h == 1:
            weights()

    def columns(x):
        hi, lo = split(x)
        return dot(gz3[...], jnp.concatenate([hi, lo, hi], axis=0))

    own_rows = pl.ds(core * 8, 8)
    other_rows = pl.ds((1 - core) * 8, 8)

    def step_zf(a, c):
        finish("a2a", a, 2, c)
        flat = bufs[a].at[3, c].reshape(1024, 128)
        ph = a // 2
        weight = wt_ref[0]

        def half(first):
            def pair(n, carry):
                r = first + n * 2
                x = jnp.concatenate([flat[pl.ds(r + e, 64, stride=16), :] for e in range(2)], axis=1)
                y = columns(x)
                for e in range(2):
                    part = y[:, e * 128 : e * 128 + 128]
                    if a == 0:
                        d_ref[c, r + e] = part
                    else:
                        part = d_ref[c, r + e] * part
                    t_ref[ph, c, r + e] = weight * jnp.log(part)
                return carry
            lax.fori_loop(0, 4, pair, 0)

        half((1 - core) * 8)
        pending["cs", ph, c] = [remote(t_ref.at[ph, c, other_rows], cb_ref.at[ph, c], device(k=1 - core))]
        half(core * 8)

    def rows_of(h, n=2, off=0):
        return pl.ds(h * 2 + off, n)

    def step_cs(a, c):
        ph = a // 2
        finish("cs", ph, c)
        u_ref[ph, c] = t_ref[ph, c, own_rows] + cb_ref[ph, c]
        pending["rs1", ph, c] = [
            remote(u_ref.at[ph, c, rows_of(far, 1, 0)], r1_ref.at[ph, c, 0], device(h=right)),
            remote(u_ref.at[ph, c, rows_of(far, 1, 1)], r1_ref.at[ph, c, 1], device(h=left)),
        ]

    def step_rs1(a, c):
        ph = a // 2
        finish("rs1", ph, c)
        u_ref[ph, c, rows_of(right, 1, 0)] += r1_ref[ph, c, 0]
        u_ref[ph, c, rows_of(left, 1, 1)] += r1_ref[ph, c, 1]
        pending["rs2", ph, c] = [
            remote(u_ref.at[ph, c, rows_of(right)], r2_ref.at[ph, c, 0], device(h=right)),
            remote(u_ref.at[ph, c, rows_of(left)], r2_ref.at[ph, c, 1], device(h=left)),
        ]

    def step_rs2(a, c):
        ph = a // 2
        if a == 0 and c == 0:
            total_weight()
        finish("rs2", ph, c)
        total = u_ref[ph, c, rows_of(zh)] + (r2_ref[ph, c, 0] + r2_ref[ph, c, 1])
        mean = jnp.exp(total * wts[6, 0:1, 0:1].reshape(1, 1, 1))
        if a == 0:
            bar_ref[c, rows_of(zh)] = mean
            here = bar_ref.at[c, rows_of(zh)]
            pending["ag1", c] = [remote(here, here, device(h=right)), remote(here, here, device(h=left))]
        else:
            flat = share_ref.at[0].reshape(512, 128)
            for e in range(2):
                flat[pl.ds(c * 2 + e, 64, stride=8), :] = mean[e]

    def step_ag1(a, c):
        finish("ag1", c)
        one = bar_ref.at[c, rows_of(left, 1, 0)]
        two = bar_ref.at[c, rows_of(right, 1, 1)]
        pending["ag2", c] = [remote(one, one, device(h=right)), remote(two, two, device(h=left))]

    def step_ag2(a, c):
        finish("ag2", c)
        pending["cg", c] = [remote(bar_ref.at[c], oth_ref.at[c], device(k=1 - core))]

    def step_zb(a, c):
        flat = b1.at[0, c].reshape(1024, 128)

        def half(src, first):
            def pair(n, carry):
                r = first + n * 2
                parts = []
                for e in range(2):
                    v = src[c, n * 2 + e] / d_ref[c, r + e]
                    d_ref[c, r + e] = v
                    parts.append(v)
                y = columns(jnp.concatenate(parts, axis=1))
                for e in range(2):
                    flat[pl.ds(r + e, 64, stride=16), :] = y[:, e * 128 : e * 128 + 128]
                return carry
            lax.fori_loop(0, 4, pair, 0)

        half(bar_ref, core * 8)
        finish("cg", c)
        half(oth_ref, (1 - core) * 8)
        start(1, 0, c)

    def step_xb(h):
        for e in range(2):
            finish("a2a", 1, 2, 2 * h + e)
        cols = slice(h * 256, h * 256 + 256)
        for p in range(2):
            x = jnp.concatenate([b1[3, 2 * h + e, p].reshape(512, 128) for e in range(2)], axis=1)
            hi, lo = split(x)
            thi[p * 512 : p * 512 + 512, :] = hi
            tlo[p * 512 : p * 512 + 512, :] = lo

            def along_x(m, carry):
                rows = pl.ds(pl.multiple_of(m * 128, 128), 128)
                to = pl.ds(pl.multiple_of(p * 512 + m * 128, 128), 128)
                k = slice(p * 512, p * 512 + 512)
                x = dot(gxh[rows, :], thi[k, :]) + (dot(gxl[rows, :], thi[k, :]) + dot(gxh[rows, :], tlo[k, :]))
                hi, lo = split(x)
                whi[to, cols] = hi
                wlo[to, cols] = lo
                return carry
            lax.fori_loop(0, 4, along_x, 0)

    def step_yb():
        def along_y(m, carry):
            rows = pl.ds(pl.multiple_of(m * 128, 128), 128)
            a_hi, a_lo = whi[rows, :], wlo[rows, :]
            x = dot(a_hi, gyh[...]) + (dot(a_lo, gyh[...]) + dot(a_hi, gyl[...]))
            w = dens_ref[rows, :] / x
            w_ref[rows, :] = w
            hi, lo = split(w)
            whi[rows, :] = hi
            wlo[rows, :] = lo
            return carry
        lax.fori_loop(0, 8, along_y, 0)
        copy = pltpu.make_async_copy(w_ref, w_hbm, io_sem.at[1])
        copy.start()
        outs.append(copy)

    def part(ref, h):
        return ref.at[..., pl.ds(h * 4, 4), :]

    def step_tx(h):
        pending["tail", h] = swap(share_ref, (0,), share_ref, (1,), "x", h)

    def step_ty(h):
        finish("tail", h)
        pending["tail", h] = swap(share_ref, (1,), share_ref, (2,), "y", h)

    def step_tz(h):
        finish("tail", h)
        pending["tail", h] = swap(share_ref, (2,), gath_ref, (core, zh), "z", h)

    def both(one, two):
        return [remote(one, one, device(h=right)), remote(two, two, device(h=left))]

    def across(h, *at):
        here = part(gath_ref.at[(core,) + at], h)
        pending["over", h].append(remote(here, here, device(k=1 - core)))

    def step_tg(h):
        finish("tail", h)
        here = part(gath_ref.at[core, zh], h)
        pending["tail", h] = both(here, here)
        pending["over", h] = []
        across(h, zh)

    def step_th(h):
        finish("tail", h)
        pending["tail", h] = both(part(gath_ref.at[core, left, 0], h), part(gath_ref.at[core, right, 1], h))
        across(h, left)
        across(h, right)

    def step_ti(h):
        finish("tail", h)
        across(h, far)

    def step_tp(h):
        def place(k):
            def block(zz, carry):
                n = k * 4 + zz
                src = gath_ref.at[k, zz].reshape(512, 128)
                for c in (2 * h, 2 * h + 1):
                    for e in range(2):
                        dst = bary_ref.at[c]
                        dst[pl.ds(n * 2 + e, 64, stride=16), :] = src[pl.ds(c * 2 + e, 64, stride=8), :]
                return carry
            lax.fori_loop(0, 4, block, 0)

        place(core)
        finish("over", h)
        place(1 - core)
        for c in (2 * h, 2 * h + 1):
            copy = pltpu.make_async_copy(bary_ref.at[c], bary_hbm.at[:, pl.ds(c * 128, 128)], io_sem.at[2 + c])
            copy.start()
            outs.append(copy)

    table = {
        "conv": step_conv, "adv": step_adv, "zf": step_zf, "cs": step_cs, "rs1": step_rs1, "rs2": step_rs2,
        "ag1": step_ag1, "ag2": step_ag2, "zb": step_zb, "xb": step_xb, "yb": step_yb,
        "tx": step_tx, "ty": step_ty, "tz": step_tz, "tg": step_tg, "th": step_th, "ti": step_ti, "tp": step_tp,
    }
    for name, *rest in ORDER:
        while len(sent) > 40:
            sent.pop(0).wait_send()
        table[name](*rest)
    for copy in sent:
        copy.wait_send()
    for copy in outs:
        copy.wait()
    assert count[0] <= SEMS and not pending


SEMS = 260


def local(densities, weights, spreads):
    field = (4, CH, 2, 4, 2, 4, 16, 128)
    vmem = pltpu.VMEM
    scratch = [
        vmem((1024, 512), F32), vmem((1024, 512), F32), vmem((CH, 1024, 128), F32), vmem((512, 128), F32),
        vmem(field, F32), vmem(field, F32), vmem(field, F32),
        vmem((CH, 16, 64, 128), F32),
        vmem((2, CH, 16, 64, 128), F32),
        vmem((2, CH, 8, 64, 128), F32),
        vmem((2, CH, 8, 64, 128), F32),
        vmem((2, CH, 2, 1, 64, 128), F32),
        vmem((2, CH, 2, 2, 64, 128), F32),
        vmem((CH, 8, 64, 128), F32),
        vmem((CH, 8, 64, 128), F32),
        vmem((3, 2, 4, 2, 4, 8, 128), F32),
        vmem((2, 4, 2, 4, 2, 4, 8, 128), F32),
        vmem((1024, 512), BF), vmem((1024, 512), BF),
        vmem((1024, 256), BF), vmem((1024, 256), BF),
        vmem((512, 512), BF), vmem((512, 512), BF), vmem((512, 512), BF), vmem((512, 512), BF),
        vmem((64, 192), BF),
        vmem((7, 8, 128), F32),
        pltpu.SemaphoreType.DMA((6,)), pltpu.SemaphoreType.DMA((SEMS,)), pltpu.SemaphoreType.DMA((SEMS,)),
    ]
    whole = pl.BlockSpec(memory_space=pl.ANY)
    smem = pl.BlockSpec(memory_space=pltpu.SMEM)
    bary, scale_w = pl.pallas_call(
        body,
        out_shape=[
            jax.ShapeDtypeStruct((1024, 512), F32),
            jax.ShapeDtypeStruct((1024, 512), F32),
        ],
        in_specs=[whole, smem, smem],
        out_specs=[whole, whole],
        scratch_shapes=scratch,
        compiler_params=pltpu.CompilerParams(
            collective_id=0, has_side_effects=True, vmem_limit_bytes=61 * 1024 * 1024
        ),
        name="sinkhorn",
    )(densities.reshape(1024, 512), weights, spreads)
    return bary.reshape(2, 512, 512), scale_w.reshape(1, 2, 512, 512)


def solution(mesh):
    return jax.shard_map(
        local,
        mesh=mesh,
        in_specs=(P("dens", "sp", None, None), P("dens"), P()),
        out_specs=(P("sp", None, None), P("dens", "sp", None, None)),
        check_vma=False,
    )
```

```python
import functools
import math

import jax
import jax.numpy as jnp
from jax import lax
from jax.experimental import pallas as pl
from jax.experimental.pallas import tpu as pltpu
from jax.sharding import PartitionSpec as P

MESH = pl.DeviceIdType.MESH
BF = jnp.bfloat16
F32 = jnp.float32

NXD, NYD, NZD, NHD = 4, 4, 2, 4
CH = 4
SIZE = {"x": NXD, "y": NYD, "z": NZD}
AXES = (
    (("yxz", "yzx"), ("zyx", "xzy"), ("yxz", "zyx"), ("xyz", "yzx")),
    (("zyx", "xyz"), ("yxz", "xyz"), ("xzy", "zyx"), ("xyz", "zxy")),
    (("yzx", "yzx"), ("zxy", "xyz"), ("xzy", "xzy"), ("yzx", "yxz")),
)


ORDER = (
    ("conv", 0, 0), ("conv", 0, 1), ("adv", 0, 0, 0, 0), ("adv", 0, 0, 1, 0), ("adv", 0, 0, 1, 1), ("adv", 0, 0, 0, 1),
    ("adv", 0, 0, 2, 1), ("adv", 0, 0, 3, 0), ("adv", 0, 0, 2, 0), ("adv", 0, 1, 0, 0), ("adv", 0, 1, 1, 1), ("adv", 0, 0, 3, 1),
    ("adv", 0, 1, 0, 1), ("adv", 0, 1, 2, 0), ("adv", 0, 1, 1, 0), ("zo", 0, 0), ("adv", 0, 1, 2, 1), ("zw", 0, 0),
    ("adv", 0, 1, 3, 1), ("cs", 0, 0), ("adv", 0, 1, 3, 0), ("zo", 0, 1), ("zo", 0, 2), ("zw", 0, 1), ("zw", 0, 2), ("cs", 0, 1),
    ("rs1", 0, 0), ("cs", 0, 2), ("zo", 0, 3), ("zw", 0, 3), ("cs", 0, 3), ("rs1", 0, 1), ("rs2", 0, 0), ("rs1", 0, 2),
    ("rs1", 0, 3), ("rs2", 0, 1), ("ag1", 0, 0), ("rs2", 0, 2), ("rs2", 0, 3), ("ag1", 0, 1), ("ag2", 0, 0), ("zbw", 0, 0),
    ("ag1", 0, 2), ("ag1", 0, 3), ("zbo", 0, 0), ("ag2", 0, 1), ("zbw", 0, 1), ("adv", 1, 0, 0, 1), ("ag2", 0, 2), ("zbw", 0, 2),
    ("zbo", 0, 1), ("adv", 1, 0, 0, 0), ("ag2", 0, 3), ("zbw", 0, 3), ("zbo", 0, 2), ("adv", 1, 0, 1, 1), ("adv", 1, 1, 0, 1),
    ("zbo", 0, 3), ("adv", 1, 0, 2, 1), ("adv", 1, 0, 1, 0), ("adv", 1, 0, 3, 1), ("adv", 1, 0, 2, 0), ("adv", 1, 1, 0, 0),
    ("adv", 1, 0, 3, 0), ("adv", 1, 1, 1, 1), ("adv", 1, 1, 2, 0), ("adv", 1, 1, 1, 0), ("adv", 1, 1, 2, 1), ("adv", 1, 1, 3, 0),
    ("adv", 1, 1, 3, 1), ("xb", 0), ("xb", 1), ("yb",), ("conv", 2, 0), ("conv", 2, 1), ("adv", 2, 0, 0, 0), ("adv", 2, 0, 1, 0),
    ("adv", 2, 0, 1, 1), ("adv", 2, 0, 0, 1), ("adv", 2, 0, 2, 0), ("adv", 2, 1, 0, 0), ("adv", 2, 0, 2, 1), ("adv", 2, 0, 3, 0),
    ("adv", 2, 1, 0, 1), ("adv", 2, 0, 3, 1), ("adv", 2, 1, 1, 0), ("adv", 2, 1, 2, 0), ("adv", 2, 1, 1, 1), ("zo", 2, 0),
    ("adv", 2, 1, 2, 1), ("zw", 2, 0), ("zo", 2, 1), ("cs", 2, 0), ("adv", 2, 1, 3, 0), ("adv", 2, 1, 3, 1), ("zo", 2, 2),
    ("zw", 2, 1), ("zw", 2, 2), ("cs", 2, 1), ("cs", 2, 2), ("rs1", 2, 0), ("zo", 2, 3), ("zw", 2, 3), ("cs", 2, 3),
    ("rs1", 2, 1), ("rs1", 2, 2), ("rs2", 2, 0), ("rs1", 2, 3), ("rs2", 2, 1), ("tx", 0), ("rs2", 2, 2), ("rs2", 2, 3), ("tx", 1),
    ("ty", 0), ("ty", 1), ("tz", 0), ("tz", 1), ("tg", 0), ("tg", 1), ("th", 0), ("th", 1), ("ti", 0), ("ti", 1), ("tp", 0),
    ("tp", 1),
)


def split(x):
    hi = x.astype(BF)
    return hi, (x - hi.astype(F32)).astype(BF)


def dot(a, b):
    return jnp.dot(a, b, preferred_element_type=F32)


def body(
    dens_hbm, wt_ref, spread_ref, bary_hbm, w_hbm,
    dens_ref, w_ref, bary_ref, inv_x, b0, b1, b2, d_ref, t_ref, cb_ref, u_ref, r1_ref, r2_ref, bar_ref, oth_ref,
    share_ref, gath_ref, whi, wlo, thi, tlo, gxh, gxl, gyh, gyl, gz3, wts, io_sem, send_sem, recv_sem,
):
    dens = lax.axis_index("dens")
    sp = lax.axis_index("sp")
    zh, core = dens // 2, lax.rem(dens, 2)
    me = {"y": sp // 8, "z": lax.rem(sp // 4, 2), "x": lax.rem(sp, 4)}

    def device(h=zh, k=core, **at):
        at = {**me, **at}
        return {"dens": h * 2 + k, "sp": (at["y"] * 2 + at["z"]) * 4 + at["x"]}

    def around(axis, k):
        return lax.rem(me[axis] + k, SIZE[axis])

    right, left = lax.rem(zh + 1, 4), lax.rem(zh + 3, 4)
    far = lax.rem(zh + 2, 4)
    zl = me["z"]
    eff = lax.rem(zl + zh, 2)
    one = device(h=lax.rem(zh + 3 + 2 * zl, 4), z=1 - zl)
    two = device(h=lax.rem(zh + 1 + 2 * zl, 4), z=1 - zl)
    gray = lax.rem(zh + zh // 2, 2)
    bit_one = (zh // 2) * (1 - eff) + gray * eff
    bit_two = gray * (1 - eff) + (zh // 2) * eff
    quarter = bit_one * 2 + bit_two
    peers = [device(**{axis: around(axis, k)}) for axis in "xyz" for k in range(1, SIZE[axis])]
    peers += [device(k=1 - core), device(h=right), device(h=left), device(h=far), one, two]

    barrier = pltpu.get_barrier_semaphore()
    for peer in peers:
        pl.semaphore_signal(barrier, 1, device_id=peer, device_id_type=MESH)

    fetch = pltpu.make_async_copy(dens_hbm, dens_ref, io_sem.at[0])
    fetch.start()
    root = math.sqrt(math.pi)

    def gauss(i, j, s):
        diff = (i - j).astype(F32) * (1.0 / s)
        return jnp.exp(-diff * diff) * (1.0 / (s * jnp.float32(root)))

    def wide(hi_ref, lo_ref, s):
        def tile(m, total):
            at = pl.multiple_of(m * 64, 64)
            i = lax.broadcasted_iota(jnp.int32, (64, 512), 0) + at
            j = lax.broadcasted_iota(jnp.int32, (64, 512), 1)
            g = gauss(i, j, s)
            hi, lo = split(g)
            hi_ref[pl.ds(at, 64), :] = hi
            lo_ref[pl.ds(at, 64), :] = lo
            if hi_ref is gxh:
                inv_x[pl.ds(at, 64), :] = jnp.broadcast_to(1.0 / jnp.sum(g, axis=1, keepdims=True), (64, 128))
                return total
            return total + jnp.sum(g, axis=0, keepdims=True)
        return lax.fori_loop(0, 8, tile, jnp.zeros((1, 512), F32))

    sum_y = wide(gyh, gyl, spread_ref[2])
    wide(gxh, gxl, spread_ref[1])

    def plane(q):
        return ((q >> 2) & 3) * 16 + (q >> 5) * 8 + (q & 3) * 2 + ((q >> 4) & 1)

    i = lax.broadcasted_iota(jnp.int32, (64, 192), 0)
    j = lax.broadcasted_iota(jnp.int32, (64, 192), 1)
    hi, lo = split(gauss(plane(i), plane(j & 63), spread_ref[0]))
    gz3[...] = jnp.where(j < 128, hi.astype(F32), lo.astype(F32)).astype(BF)

    planes = sp * 2 + lax.broadcasted_iota(jnp.int32, (8, 128), 0)
    others = lax.broadcasted_iota(jnp.int32, (8, 128), 1)
    near = jnp.where(others < 64, gauss(planes, others, spread_ref[0]), 0.0)
    sum_z = jnp.sum(near, axis=1, keepdims=True)

    fetch.wait()
    for p in range(2):
        inv_y = 1.0 / (sum_y * sum_z[p : p + 1, :])

        def first(m, carry):
            rows = pl.ds(pl.multiple_of(p * 512 + m * 64, 64), 64)
            inv = inv_x[pl.ds(pl.multiple_of(m * 64, 64), 64), :]
            hi, lo = split(dens_ref[rows, :] * jnp.concatenate([inv] * 4, axis=1) * inv_y)
            whi[rows, :] = hi
            wlo[rows, :] = lo
            return carry
        lax.fori_loop(0, 8, first, 0)

    pl.semaphore_wait(barrier, len(peers))

    sent = []
    outs = []
    count = [0]
    turn = [0]

    def remote(src, dst, to):
        n = count[0]
        count[0] += 1
        if len(sent) >= LIVE:
            sent.pop(0).wait_send()
        turn[0] = (turn[0] + 1) % LIVE
        copy = pltpu.make_async_remote_copy(
            src, dst, send_sem.at[turn[0]], recv_sem.at[n], device_id=to, device_id_type=MESH
        )
        copy.start()
        sent.append(copy)
        return copy.wait_recv

    def local(src, dst):
        n = count[0]
        count[0] += 1
        copy = pltpu.make_async_copy(src, dst, recv_sem.at[n])
        copy.start()
        return copy.wait

    pending = {}

    def finish(*key):
        for wait in pending.pop(key):
            wait()

    own_rows = pl.ds(pl.multiple_of(core * 8, 8), 8)
    other_rows = pl.ds(pl.multiple_of((1 - core) * 8, 8), 8)

    def slot(ref, lead, axis, k, rows):
        at = [slice(None)] * 4
        at["zpyx".index(axis)] = k
        return ref.at[(*lead, *at, rows)]

    def swap(src, s_lead, dst, d_lead, axis, rows, forward):
        waits = []
        for k in range(SIZE[axis]):
            to = around(axis, k)
            take, put = to, me[axis]
            if axis == "z":
                take, put = (lax.rem(eff + k, 2), zl) if forward else (to, eff)
            pair = slot(src, s_lead, axis, take, rows), slot(dst, d_lead, axis, put, rows)
            waits.append(remote(*pair, device(**{axis: to})) if k else local(*pair))
        return waits

    bufs = (b0, b1, b2)

    def start(a, j, c, u):
        rows = own_rows if u else other_rows
        pending["a2a", a, j, c, u] = swap(bufs[a], (j, c), bufs[a], (j + 1, c), AXES[a][c][u][j], rows, a != 1)

    wts[0] = jnp.full((8, 128), wt_ref[0], F32)
    pending["wc",] = [remote(wts.at[0], wts.at[1], device(k=1 - core))]

    def weights():
        finish("wc")
        wts[2] = wts[0] + wts[1]
        pending["wh",] = [
            remote(wts.at[2], wts.at[2 + k], device(h=lax.rem(zh + k, 4))) for k in range(1, 4)
        ]

    def total_weight():
        finish("wh")
        wts[6] = 1.0 / (wts[2] + wts[3] + (wts[4] + wts[5]))

    def step_adv(a, j, c, u):
        finish("a2a", a, j, c, u)
        start(a, j + 1, c, u)

    def step_conv(a, h):
        cols = slice(h * 256, h * 256 + 256)

        def along_y(m, carry):
            rows = pl.ds(pl.multiple_of(m * 256, 256), 256)
            x = dot(whi[rows, :], gyh[:, cols]) + (dot(wlo[rows, :], gyh[:, cols]) + dot(whi[rows, :], gyl[:, cols]))
            hi, lo = split(x)
            thi[rows, :] = hi
            tlo[rows, :] = lo
            return carry
        lax.fori_loop(0, 4, along_y, 0)

        for p in range(2):
            def along_x(m, carry):
                rows = pl.ds(pl.multiple_of(m * 128, 128), 128)
                k = slice(p * 512, p * 512 + 512)
                x = dot(gxh[rows, :], thi[k, :]) + (dot(gxl[rows, :], thi[k, :]) + dot(gxh[rows, :], tlo[k, :]))
                for e in range(2):
                    bufs[a][0, 2 * h + e, :, p, m] = x[:, e * 128 : e * 128 + 128].reshape(2, 4, 16, 128)
                return carry
            lax.fori_loop(0, 4, along_x, 0)
        for e in range(2):
            start(a, 0, 2 * h + e, 0)
            start(a, 0, 2 * h + e, 1)
        if a == 0 and h == 1:
            weights()

    def columns(x):
        hi, lo = split(x)
        return dot(gz3[...], jnp.concatenate([hi, lo, hi], axis=0))

    def convolved(a, c, first):
        flat = bufs[a].at[3, c].reshape(1024, 128)
        weight = wt_ref[0]

        def pair(n, carry):
            r = first + n * 2
            x = jnp.concatenate([flat[pl.ds(r + e, 64, stride=16), :] for e in range(2)], axis=1)
            y = columns(x)
            for e in range(2):
                part = y[:, e * 128 : e * 128 + 128]
                if a == 0:
                    d_ref[c, r + e] = part
                else:
                    part = d_ref[c, r + e] * part
                t_ref[a // 2, c, r + e] = weight * jnp.log(part)
            return carry
        lax.fori_loop(0, 4, pair, 0)

    def step_zo(a, c):
        ph = a // 2
        finish("a2a", a, 2, c, 0)
        convolved(a, c, (1 - core) * 8)
        pending["cs", ph, c] = [remote(t_ref.at[ph, c, other_rows], cb_ref.at[ph, c], device(k=1 - core))]

    def step_zw(a, c):
        finish("a2a", a, 2, c, 1)
        convolved(a, c, core * 8)

    mine = pl.ds(quarter * 2, 2)
    given = pl.ds(bit_one * 4 + (1 - bit_two) * 2, 2)
    half_mine = pl.ds(bit_one * 4, 4)
    half_given = pl.ds((1 - bit_one) * 4, 4)

    def step_cs(a, c):
        ph = a // 2
        finish("cs", ph, c)
        u_ref[ph, c] = t_ref[ph, c, own_rows] + cb_ref[ph, c]
        pending["rs1", ph, c] = [remote(u_ref.at[ph, c, half_given], r1_ref.at[ph, c], one)]

    def step_rs1(a, c):
        ph = a // 2
        finish("rs1", ph, c)
        u_ref[ph, c, half_mine] += r1_ref[ph, c]
        pending["rs2", ph, c] = [remote(u_ref.at[ph, c, given], r2_ref.at[ph, c], two)]

    def step_rs2(a, c):
        ph = a // 2
        if ("wh",) in pending:
            total_weight()
        finish("rs2", ph, c)
        total = u_ref[ph, c, mine] + r2_ref[ph, c]
        mean = jnp.exp(total * wts[6, 0:1, 0:1].reshape(1, 1, 1))
        if a == 0:
            bar_ref[c, mine] = mean
            here = bar_ref.at[c, mine]
            pending["ag1", c] = [remote(here, here, two)]
        else:
            flat = share_ref.at[0].reshape(512, 128)
            for e in range(2):
                flat[pl.ds(c * 2 + e, 64, stride=8), :] = mean[e]

    def step_ag1(a, c):
        finish("ag1", c)
        here = bar_ref.at[c, half_mine]
        pending["ag2", c] = [remote(here, here, one)]

    def step_ag2(a, c):
        finish("ag2", c)
        pending["cg", c] = [remote(bar_ref.at[c], oth_ref.at[c], device(k=1 - core))]

    def scaled(src, c, first):
        flat = b1.at[0, c].reshape(1024, 128)

        def pair(n, carry):
            r = first + n * 2
            parts = []
            for e in range(2):
                v = src[c, n * 2 + e] / d_ref[c, r + e]
                d_ref[c, r + e] = v
                parts.append(v)
            y = columns(jnp.concatenate(parts, axis=1))
            for e in range(2):
                flat[pl.ds(r + e, 64, stride=16), :] = y[:, e * 128 : e * 128 + 128]
            return carry
        lax.fori_loop(0, 4, pair, 0)

    def step_zbw(a, c):
        scaled(bar_ref, c, core * 8)
        start(1, 0, c, 1)

    def step_zbo(a, c):
        finish("cg", c)
        scaled(oth_ref, c, (1 - core) * 8)
        start(1, 0, c, 0)

    def step_xb(h):
        for e in range(2):
            finish("a2a", 1, 2, 2 * h + e, 0)
            finish("a2a", 1, 2, 2 * h + e, 1)
        cols = slice(h * 256, h * 256 + 256)
        for p in range(2):
            x = jnp.concatenate(
                [
                    jnp.concatenate([b1[3, 2 * h + e, k % 2, p, k // 2].reshape(64, 128) for k in range(8)], axis=0)
                    for e in range(2)
                ],
                axis=1,
            )
            hi, lo = split(x)
            thi[p * 512 : p * 512 + 512, :] = hi
            tlo[p * 512 : p * 512 + 512, :] = lo

            def along_x(m, carry):
                rows = pl.ds(pl.multiple_of(m * 128, 128), 128)
                to = pl.ds(pl.multiple_of(p * 512 + m * 128, 128), 128)
                k = slice(p * 512, p * 512 + 512)
                x = dot(gxh[rows, :], thi[k, :]) + (dot(gxl[rows, :], thi[k, :]) + dot(gxh[rows, :], tlo[k, :]))
                hi, lo = split(x)
                whi[to, cols] = hi
                wlo[to, cols] = lo
                return carry
            lax.fori_loop(0, 4, along_x, 0)

    def step_yb():
        def along_y(m, carry):
            rows = pl.ds(pl.multiple_of(m * 128, 128), 128)
            a_hi, a_lo = whi[rows, :], wlo[rows, :]
            x = dot(a_hi, gyh[...]) + (dot(a_lo, gyh[...]) + dot(a_hi, gyl[...]))
            w = dens_ref[rows, :] / x
            w_ref[rows, :] = w
            hi, lo = split(w)
            whi[rows, :] = hi
            wlo[rows, :] = lo
            return carry
        lax.fori_loop(0, 8, along_y, 0)
        copy = pltpu.make_async_copy(w_ref, w_hbm, io_sem.at[1])
        copy.start()
        outs.append(copy)

    def part(ref, h):
        return ref.at[..., pl.ds(h * 4, 4), :]

    def step_tx(h):
        pending["tail", h] = swap(share_ref, (0,), share_ref, (1,), "x", pl.ds(h * 4, 4), False)

    def step_ty(h):
        finish("tail", h)
        pending["tail", h] = swap(share_ref, (1,), share_ref, (2,), "y", pl.ds(h * 4, 4), False)

    def step_tz(h):
        finish("tail", h)
        pending["tail", h] = swap(share_ref, (2,), gath_ref, (core, zh), "z", pl.ds(h * 4, 4), False)

    def both(to_right, to_left):
        return [remote(to_right, to_right, device(h=right)), remote(to_left, to_left, device(h=left))]

    def across(h, *at):
        here = part(gath_ref.at[(core,) + at], h)
        pending["over", h].append(remote(here, here, device(k=1 - core)))

    def step_tg(h):
        finish("tail", h)
        here = part(gath_ref.at[core, zh], h)
        pending["tail", h] = both(here, here)
        pending["over", h] = []
        across(h, zh)

    def step_th(h):
        finish("tail", h)
        pending["tail", h] = both(part(gath_ref.at[core, left, 0], h), part(gath_ref.at[core, right, 1], h))
        across(h, left)
        across(h, right)

    def step_ti(h):
        finish("tail", h)
        across(h, far)

    def step_tp(h):
        def place(k):
            for h_from in range(NHD):
                for z in range(2):
                    src = gath_ref.at[k, h_from, z].reshape(256, 128)
                    bits = h_from // 2, (h_from + h_from // 2) % 2
                    row = bits[z] * 4 + bits[1 - z] * 2
                    for c in (2 * h, 2 * h + 1):
                        dst = bary_ref.at[c, z]
                        for e in range(2):
                            dst[pl.ds(k * 8 + row + e, 32, stride=16), :] = src[pl.ds(c * 2 + e, 32, stride=8), :]

        place(core)
        finish("over", h)
        place(1 - core)
        for c in (2 * h, 2 * h + 1):
            for z in range(2):
                copy = pltpu.make_async_copy(
                    bary_ref.at[c, z].reshape(8, 64, 128), bary_hbm.at[:, z, :, pl.ds(c * 128, 128)], io_sem.at[2 + 2 * c + z]
                )
                copy.start()
                outs.append(copy)

    table = {
        "conv": step_conv, "adv": step_adv, "zo": step_zo, "zw": step_zw, "cs": step_cs, "rs1": step_rs1, "rs2": step_rs2,
        "ag1": step_ag1, "ag2": step_ag2, "zbw": step_zbw, "zbo": step_zbo, "xb": step_xb, "yb": step_yb,
        "tx": step_tx, "ty": step_ty, "tz": step_tz, "tg": step_tg, "th": step_th, "ti": step_ti, "tp": step_tp,
    }
    for name, *rest in ORDER:
        table[name](*rest)
    for copy in sent:
        copy.wait_send()
    for copy in outs:
        copy.wait()
    assert count[0] <= SEMS and not pending


SEMS = 330
LIVE = 100


def local(densities, weights, spreads):
    field = (4, CH, 2, 2, 4, 4, 16, 128)
    vmem = pltpu.VMEM
    scratch = [
        vmem((1024, 512), F32), vmem((1024, 512), F32), vmem((CH, 2, 512, 128), F32), vmem((512, 128), F32),
        vmem(field, F32), vmem(field, F32), vmem(field, F32),
        vmem((CH, 16, 64, 128), F32),
        vmem((2, CH, 16, 64, 128), F32),
        vmem((2, CH, 8, 64, 128), F32),
        vmem((2, CH, 8, 64, 128), F32),
        vmem((2, CH, 4, 64, 128), F32),
        vmem((2, CH, 2, 64, 128), F32),
        vmem((CH, 8, 64, 128), F32),
        vmem((CH, 8, 64, 128), F32),
        vmem((3, 2, 2, 4, 4, 8, 128), F32),
        vmem((2, 4, 2, 2, 4, 4, 8, 128), F32),
        vmem((1024, 512), BF), vmem((1024, 512), BF),
        vmem((1024, 256), BF), vmem((1024, 256), BF),
        vmem((512, 512), BF), vmem((512, 512), BF), vmem((512, 512), BF), vmem((512, 512), BF),
        vmem((64, 192), BF),
        vmem((7, 8, 128), F32),
        pltpu.SemaphoreType.DMA((10,)), pltpu.SemaphoreType.DMA((LIVE,)), pltpu.SemaphoreType.DMA((SEMS,)),
    ]
    whole = pl.BlockSpec(memory_space=pl.ANY)
    smem = pl.BlockSpec(memory_space=pltpu.SMEM)
    bary, scale_w = pl.pallas_call(
        body,
        out_shape=[
            jax.ShapeDtypeStruct((8, 2, 64, 512), F32),
            jax.ShapeDtypeStruct((1024, 512), F32),
        ],
        in_specs=[whole, smem, smem],
        out_specs=[whole, whole],
        scratch_shapes=scratch,
        compiler_params=pltpu.CompilerParams(
            collective_id=0, has_side_effects=True, vmem_limit_bytes=61 * 1024 * 1024
        ),
        name="sinkhorn",
    )(densities.reshape(1024, 512), weights, spreads)
    return bary.reshape(2, 512, 512), scale_w.reshape(1, 2, 512, 512)


def solution(mesh):
    return jax.shard_map(
        local,
        mesh=mesh,
        in_specs=(P("dens", "sp", None, None), P("dens"), P()),
        out_specs=(P("sp", None, None), P("dens", "sp", None, None)),
        check_vma=False,
    )
```

```python
import itertools
import math

import jax
import jax.numpy as jnp
from jax import lax
from jax.experimental import pallas as pl
from jax.experimental.pallas import tpu as pltpu
from jax.sharding import PartitionSpec as P

MESH = pl.DeviceIdType.MESH
BF = jnp.bfloat16
F32 = jnp.float32

NXD, NYD, NZD, NHD = 4, 4, 2, 4
CH = 4
SIZE = {"x": NXD, "y": NYD, "z": NZD}
AXES = (
    ((("x", "yz"), ("x", "yz")), (("x", "yz"), ("yz", "x")), (("yz", "x"), ("x", "yz")), (("x", "yz"), ("x", "yz"))),
    ((("x", "yz"), ("x", "yz")), (("x", "yz"), ("x", "yz")), (("x", "yz"), ("yz", "x")), (("x", "yz"), ("yz", "x"))),
    ((("yz", "x"), ("yz", "x")), (("yz", "x"), ("x", "yz")), (("yz", "x"), ("x", "yz")), (("yz", "x"), ("yz", "x"))),
)


ORDER = (
    ("conv", 0, 0), ("conv", 0, 1), ("adv", 0, 0, 0, 0), ("adv", 0, 0, 1, 1), ("adv", 0, 0, 0, 1), ("adv", 0, 0, 2, 0),
    ("adv", 0, 0, 1, 0), ("zo", 0, 0), ("adv", 0, 0, 2, 1), ("zw", 0, 0), ("cs", 0, 0), ("adv", 0, 0, 3, 0), ("zo", 0, 1),
    ("adv", 0, 0, 3, 1), ("zw", 0, 2), ("rs1", 0, 0), ("zw", 0, 1), ("zo", 0, 3), ("cs", 0, 1), ("zo", 0, 2), ("zw", 0, 3),
    ("rs2", 0, 0), ("cs", 0, 3), ("cs", 0, 2), ("rs1", 0, 1), ("ag1", 0, 0), ("rs1", 0, 3), ("rs1", 0, 2), ("rs2", 0, 1),
    ("ag2", 0, 0), ("zbw", 0, 0), ("rs2", 0, 3), ("rs2", 0, 2), ("zbo", 0, 0), ("ag1", 0, 1), ("ag1", 0, 3), ("adv", 1, 0, 0, 1),
    ("ag1", 0, 2), ("adv", 1, 0, 0, 0), ("ag2", 0, 1), ("zbw", 0, 1), ("ag2", 0, 3), ("zbw", 0, 3), ("zbo", 0, 1), ("ag2", 0, 2),
    ("zbw", 0, 2), ("zbo", 0, 3), ("adv", 1, 0, 1, 1), ("zbo", 0, 2), ("adv", 1, 0, 3, 1), ("adv", 1, 0, 1, 0),
    ("adv", 1, 0, 2, 1), ("adv", 1, 0, 3, 0), ("adv", 1, 0, 2, 0), ("xb", 0), ("xb", 1), ("yb",), ("conv", 2, 0), ("conv", 2, 1),
    ("adv", 2, 0, 0, 0), ("adv", 2, 0, 1, 1), ("adv", 2, 0, 0, 1), ("adv", 2, 0, 2, 1), ("adv", 2, 0, 1, 0), ("zo", 2, 0),
    ("adv", 2, 0, 2, 0), ("zw", 2, 0), ("cs", 2, 0), ("adv", 2, 0, 3, 0), ("zo", 2, 1), ("adv", 2, 0, 3, 1), ("zo", 2, 2),
    ("rs1", 2, 0), ("zw", 2, 1), ("zo", 2, 3), ("cs", 2, 1), ("zw", 2, 2), ("zw", 2, 3), ("cs", 2, 2), ("rs2", 2, 0),
    ("cs", 2, 3), ("rs1", 2, 1), ("rs1", 2, 2), ("rs1", 2, 3), ("rs2", 2, 1), ("tx", 0), ("rs2", 2, 2), ("rs2", 2, 3), ("tx", 1),
    ("ty", 0), ("ty", 1), ("tg", 0), ("tg", 1), ("th", 0), ("th", 1), ("ti", 0), ("ti", 1), ("tp", 0), ("tp", 1),
)


def split(x):
    hi = x.astype(BF)
    return hi, (x - hi.astype(F32)).astype(BF)


def dot(a, b):
    return jnp.dot(a, b, preferred_element_type=F32)


def body(
    dens_hbm, wt_ref, spread_ref, bary_hbm, w_hbm,
    dens_ref, w_ref, bary_ref, inv_x, b0, b1, b2, d_ref, t_ref, cb_ref, u_ref, r1_ref, r2_ref, bar_ref, oth_ref,
    share_ref, gath_ref, whi, wlo, thi, tlo, gxh, gxl, gyh, gyl, gz3, wts, io_sem, send_sem, recv_sem,
):
    dens = lax.axis_index("dens")
    sp = lax.axis_index("sp")
    zh, core = dens // 2, lax.rem(dens, 2)
    me = {"y": sp // 8, "z": lax.rem(sp // 4, 2), "x": lax.rem(sp, 4)}

    def device(h=zh, k=core, **at):
        at = {**me, **at}
        return {"dens": h * 2 + k, "sp": (at["y"] * 2 + at["z"]) * 4 + at["x"]}

    def around(axis, k):
        return lax.rem(me[axis] + k, SIZE[axis])

    right, left = lax.rem(zh + 1, 4), lax.rem(zh + 3, 4)
    far = lax.rem(zh + 2, 4)
    zl = me["z"]
    eff = lax.rem(zl + zh, 2)
    one = device(h=lax.rem(zh + 3 + 2 * zl, 4), z=1 - zl)
    two = device(h=lax.rem(zh + 1 + 2 * zl, 4), z=1 - zl)
    gray = lax.rem(zh + zh // 2, 2)
    bit_one = (zh // 2) * (1 - eff) + gray * eff
    bit_two = gray * (1 - eff) + (zh // 2) * eff
    quarter = bit_one * 2 + bit_two
    peers = [device(**{axis: around(axis, k)}) for axis in "xyz" for k in range(1, SIZE[axis])]
    peers += [device(y=around("y", k), z=around("z", 1)) for k in range(1, NYD)]
    peers += [device(k=1 - core), device(h=right), device(h=left), device(h=far), one, two]

    barrier = pltpu.get_barrier_semaphore()
    for peer in peers:
        pl.semaphore_signal(barrier, 1, device_id=peer, device_id_type=MESH)

    fetch = pltpu.make_async_copy(dens_hbm, dens_ref, io_sem.at[0])
    fetch.start()
    root = math.sqrt(math.pi)

    def gauss(i, j, s):
        diff = (i - j).astype(F32) * (1.0 / s)
        return jnp.exp(-diff * diff) * (1.0 / (s * jnp.float32(root)))

    def wide(hi_ref, lo_ref, s):
        def tile(m, total):
            at = pl.multiple_of(m * 64, 64)
            i = lax.broadcasted_iota(jnp.int32, (64, 512), 0) + at
            j = lax.broadcasted_iota(jnp.int32, (64, 512), 1)
            g = gauss(i, j, s)
            hi, lo = split(g)
            hi_ref[pl.ds(at, 64), :] = hi
            lo_ref[pl.ds(at, 64), :] = lo
            if hi_ref is gxh:
                inv_x[pl.ds(at, 64), :] = jnp.broadcast_to(1.0 / jnp.sum(g, axis=1, keepdims=True), (64, 128))
                return total
            return total + jnp.sum(g, axis=0, keepdims=True)
        return lax.fori_loop(0, 8, tile, jnp.zeros((1, 512), F32))

    sum_y = wide(gyh, gyl, spread_ref[2])
    wide(gxh, gxl, spread_ref[1])

    def plane(q):
        return ((q >> 2) & 3) * 16 + (q >> 5) * 8 + (q & 3) * 2 + ((q >> 4) & 1)

    i = lax.broadcasted_iota(jnp.int32, (64, 192), 0)
    j = lax.broadcasted_iota(jnp.int32, (64, 192), 1)
    hi, lo = split(gauss(plane(i), plane(j & 63), spread_ref[0]))
    gz3[...] = jnp.where(j < 128, hi.astype(F32), lo.astype(F32)).astype(BF)

    planes = sp * 2 + lax.broadcasted_iota(jnp.int32, (8, 128), 0)
    others = lax.broadcasted_iota(jnp.int32, (8, 128), 1)
    near = jnp.where(others < 64, gauss(planes, others, spread_ref[0]), 0.0)
    sum_z = jnp.sum(near, axis=1, keepdims=True)

    fetch.wait()
    for p in range(2):
        inv_y = 1.0 / (sum_y * sum_z[p : p + 1, :])

        def first(m, carry):
            rows = pl.ds(pl.multiple_of(p * 512 + m * 64, 64), 64)
            inv = inv_x[pl.ds(pl.multiple_of(m * 64, 64), 64), :]
            hi, lo = split(dens_ref[rows, :] * jnp.concatenate([inv] * 4, axis=1) * inv_y)
            whi[rows, :] = hi
            wlo[rows, :] = lo
            return carry
        lax.fori_loop(0, 8, first, 0)

    pl.semaphore_wait(barrier, len(peers))

    sent = []
    outs = []
    count = [0]
    turn = [0]

    def remote(src, dst, to):
        n = count[0]
        count[0] += 1
        if len(sent) >= LIVE:
            sent.pop(0).wait_send()
        turn[0] = (turn[0] + 1) % LIVE
        copy = pltpu.make_async_remote_copy(
            src, dst, send_sem.at[turn[0]], recv_sem.at[n], device_id=to, device_id_type=MESH
        )
        copy.start()
        sent.append(copy)
        return copy.wait_recv

    def local(src, dst):
        n = count[0]
        count[0] += 1
        copy = pltpu.make_async_copy(src, dst, recv_sem.at[n])
        copy.start()
        return copy.wait

    pending = {}

    def finish(*key):
        for wait in pending.pop(key):
            wait()

    own_rows = pl.ds(pl.multiple_of(core * 8, 8), 8)
    other_rows = pl.ds(pl.multiple_of((1 - core) * 8, 8), 8)

    def slot(ref, lead, at, rows):
        at = tuple(at.get(axis, slice(None)) for axis in "zpyx")
        return ref.at[(*lead, *at) if rows is None else (*lead, *at, rows)]

    def swap(src, s_lead, dst, d_lead, axes, rows, forward):
        waits = []
        for ks in itertools.product(*(range(SIZE[axis]) for axis in axes)):
            to = {axis: around(axis, k) for axis, k in zip(axes, ks)}
            take, put = dict(to), {axis: me[axis] for axis in axes}
            if "z" in axes:
                if forward:
                    take["z"] = lax.rem(eff + ks[axes.index("z")], 2)
                else:
                    put["z"] = eff
            pair = slot(src, s_lead, take, rows), slot(dst, d_lead, put, rows)
            waits.append(remote(*pair, device(**to)) if any(ks) else local(*pair))
        return waits

    bufs = (b0, b1, b2)

    def start(a, j, c, u):
        half = core if u else 1 - core
        pending["a2a", a, j, c, u] = swap(
            bufs[a], (j, c, half), bufs[a], (j + 1, c, half), AXES[a][c][u][j], None, a != 1
        )

    wts[0] = jnp.full((8, 128), wt_ref[0], F32)
    pending["wc",] = [remote(wts.at[0], wts.at[1], device(k=1 - core))]

    def weights():
        finish("wc")
        wts[2] = wts[0] + wts[1]
        pending["wh",] = [
            remote(wts.at[2], wts.at[2 + k], device(h=lax.rem(zh + k, 4))) for k in range(1, 4)
        ]

    def total_weight():
        finish("wh")
        wts[6] = 1.0 / (wts[2] + wts[3] + (wts[4] + wts[5]))

    def step_adv(a, j, c, u):
        finish("a2a", a, j, c, u)
        start(a, j + 1, c, u)

    def step_conv(a, h):
        cols = slice(h * 256, h * 256 + 256)

        def along_y(m, carry):
            rows = pl.ds(pl.multiple_of(m * 256, 256), 256)
            x = dot(whi[rows, :], gyh[:, cols]) + (dot(wlo[rows, :], gyh[:, cols]) + dot(whi[rows, :], gyl[:, cols]))
            hi, lo = split(x)
            thi[rows, :] = hi
            tlo[rows, :] = lo
            return carry
        lax.fori_loop(0, 4, along_y, 0)

        for p in range(2):
            def along_x(m, carry):
                rows = pl.ds(pl.multiple_of(m * 128, 128), 128)
                k = slice(p * 512, p * 512 + 512)
                x = dot(gxh[rows, :], thi[k, :]) + (dot(gxl[rows, :], thi[k, :]) + dot(gxh[rows, :], tlo[k, :]))
                for e in range(2):
                    block = x[:, e * 128 : e * 128 + 128].reshape(2, 4, 2, 8, 128)
                    for half in range(2):
                        bufs[a][0, 2 * h + e, half, :, p, m] = block[:, :, half]
                return carry
            lax.fori_loop(0, 4, along_x, 0)
        for e in range(2):
            start(a, 0, 2 * h + e, 0)
            start(a, 0, 2 * h + e, 1)
        if a == 0 and h == 1:
            weights()

    def columns(x):
        hi, lo = split(x)
        return dot(gz3[...], jnp.concatenate([hi, lo, hi], axis=0))

    def convolved(a, c, half):
        flat = bufs[a].at[2, c, half].reshape(512, 128)
        weight = wt_ref[0]

        def pair(n, carry):
            r = half * 8 + n * 2
            x = jnp.concatenate([flat[pl.ds(n * 2 + e, 64, stride=8), :] for e in range(2)], axis=1)
            y = columns(x)
            for e in range(2):
                part = y[:, e * 128 : e * 128 + 128]
                if a == 0:
                    d_ref[c, r + e] = part
                else:
                    part = d_ref[c, r + e] * part
                t_ref[a // 2, c, r + e] = weight * jnp.log(part)
            return carry
        lax.fori_loop(0, 4, pair, 0)

    def step_zo(a, c):
        ph = a // 2
        finish("a2a", a, 1, c, 0)
        convolved(a, c, 1 - core)
        pending["cs", ph, c] = [remote(t_ref.at[ph, c, other_rows], cb_ref.at[ph, c], device(k=1 - core))]

    def step_zw(a, c):
        finish("a2a", a, 1, c, 1)
        convolved(a, c, core)

    mine = pl.ds(quarter * 2, 2)
    given = pl.ds(bit_one * 4 + (1 - bit_two) * 2, 2)
    half_mine = pl.ds(bit_one * 4, 4)
    half_given = pl.ds((1 - bit_one) * 4, 4)

    def step_cs(a, c):
        ph = a // 2
        finish("cs", ph, c)
        u_ref[ph, c] = t_ref[ph, c, own_rows] + cb_ref[ph, c]
        pending["rs1", ph, c] = [remote(u_ref.at[ph, c, half_given], r1_ref.at[ph, c], one)]

    def step_rs1(a, c):
        ph = a // 2
        finish("rs1", ph, c)
        u_ref[ph, c, half_mine] += r1_ref[ph, c]
        pending["rs2", ph, c] = [remote(u_ref.at[ph, c, given], r2_ref.at[ph, c], two)]

    def step_rs2(a, c):
        ph = a // 2
        if ("wh",) in pending:
            total_weight()
        finish("rs2", ph, c)
        total = u_ref[ph, c, mine] + r2_ref[ph, c]
        mean = jnp.exp(total * wts[6, 0:1, 0:1].reshape(1, 1, 1))
        if a == 0:
            bar_ref[c, mine] = mean
            here = bar_ref.at[c, mine]
            pending["ag1", c] = [remote(here, here, two)]
        else:
            flat = share_ref.at[0].reshape(512, 128)
            for e in range(2):
                flat[pl.ds(c * 2 + e, 64, stride=8), :] = mean[e]

    def step_ag1(a, c):
        finish("ag1", c)
        here = bar_ref.at[c, half_mine]
        pending["ag2", c] = [remote(here, here, one)]

    def step_ag2(a, c):
        finish("ag2", c)
        pending["cg", c] = [remote(bar_ref.at[c], oth_ref.at[c], device(k=1 - core))]

    def scaled(src, c, half):
        flat = b1.at[0, c, half].reshape(512, 128)

        def pair(n, carry):
            r = half * 8 + n * 2
            parts = []
            for e in range(2):
                v = src[c, n * 2 + e] / d_ref[c, r + e]
                d_ref[c, r + e] = v
                parts.append(v)
            y = columns(jnp.concatenate(parts, axis=1))
            for e in range(2):
                flat[pl.ds(n * 2 + e, 64, stride=8), :] = y[:, e * 128 : e * 128 + 128]
            return carry
        lax.fori_loop(0, 4, pair, 0)

    def step_zbw(a, c):
        scaled(bar_ref, c, core)
        start(1, 0, c, 1)

    def step_zbo(a, c):
        finish("cg", c)
        scaled(oth_ref, c, 1 - core)
        start(1, 0, c, 0)

    def step_xb(h):
        for e in range(2):
            finish("a2a", 1, 1, 2 * h + e, 0)
            finish("a2a", 1, 1, 2 * h + e, 1)
        cols = slice(h * 256, h * 256 + 256)
        for p in range(2):
            def block(c, k):
                halves = [b1[2, c, half, k % 2, p, k // 2][:, None] for half in range(2)]
                return jnp.concatenate(halves, axis=1).reshape(64, 128)

            x = jnp.concatenate(
                [jnp.concatenate([block(2 * h + e, k) for k in range(8)], axis=0) for e in range(2)], axis=1
            )
            hi, lo = split(x)
            thi[p * 512 : p * 512 + 512, :] = hi
            tlo[p * 512 : p * 512 + 512, :] = lo

            def along_x(m, carry):
                rows = pl.ds(pl.multiple_of(m * 128, 128), 128)
                to = pl.ds(pl.multiple_of(p * 512 + m * 128, 128), 128)
                k = slice(p * 512, p * 512 + 512)
                x = dot(gxh[rows, :], thi[k, :]) + (dot(gxl[rows, :], thi[k, :]) + dot(gxh[rows, :], tlo[k, :]))
                hi, lo = split(x)
                whi[to, cols] = hi
                wlo[to, cols] = lo
                return carry
            lax.fori_loop(0, 4, along_x, 0)

    def step_yb():
        def along_y(m, carry):
            rows = pl.ds(pl.multiple_of(m * 128, 128), 128)
            a_hi, a_lo = whi[rows, :], wlo[rows, :]
            x = dot(a_hi, gyh[...]) + (dot(a_lo, gyh[...]) + dot(a_hi, gyl[...]))
            w = dens_ref[rows, :] / x
            w_ref[rows, :] = w
            hi, lo = split(w)
            whi[rows, :] = hi
            wlo[rows, :] = lo
            return carry
        lax.fori_loop(0, 8, along_y, 0)
        copy = pltpu.make_async_copy(w_ref, w_hbm, io_sem.at[1])
        copy.start()
        outs.append(copy)

    def part(ref, h):
        return ref.at[..., pl.ds(h * 4, 4), :]

    def step_tx(h):
        pending["tail", h] = swap(share_ref, (0,), share_ref, (1,), "x", pl.ds(h * 4, 4), False)

    def step_ty(h):
        finish("tail", h)
        pending["tail", h] = swap(share_ref, (1,), gath_ref, (core, zh), "yz", pl.ds(h * 4, 4), False)

    def both(to_right, to_left):
        return [remote(to_right, to_right, device(h=right)), remote(to_left, to_left, device(h=left))]

    def across(h, *at):
        here = part(gath_ref.at[(core,) + at], h)
        pending["over", h].append(remote(here, here, device(k=1 - core)))

    def step_tg(h):
        finish("tail", h)
        here = part(gath_ref.at[core, zh], h)
        pending["tail", h] = both(here, here)
        pending["over", h] = []
        across(h, zh)

    def step_th(h):
        finish("tail", h)
        pending["tail", h] = both(part(gath_ref.at[core, left, 0], h), part(gath_ref.at[core, right, 1], h))
        across(h, left)
        across(h, right)

    def step_ti(h):
        finish("tail", h)
        across(h, far)

    def step_tp(h):
        def place(k):
            for h_from in range(NHD):
                for z in range(2):
                    src = gath_ref.at[k, h_from, z].reshape(256, 128)
                    bits = h_from // 2, (h_from + h_from // 2) % 2
                    row = bits[z] * 4 + bits[1 - z] * 2
                    for c in (2 * h, 2 * h + 1):
                        dst = bary_ref.at[c, z]
                        for e in range(2):
                            dst[pl.ds(k * 8 + row + e, 32, stride=16), :] = src[pl.ds(c * 2 + e, 32, stride=8), :]

        place(core)
        finish("over", h)
        place(1 - core)
        for c in (2 * h, 2 * h + 1):
            for z in range(2):
                copy = pltpu.make_async_copy(
                    bary_ref.at[c, z].reshape(8, 64, 128), bary_hbm.at[:, z, :, pl.ds(c * 128, 128)], io_sem.at[2 + 2 * c + z]
                )
                copy.start()
                outs.append(copy)

    table = {
        "conv": step_conv, "adv": step_adv, "zo": step_zo, "zw": step_zw, "cs": step_cs, "rs1": step_rs1, "rs2": step_rs2,
        "ag1": step_ag1, "ag2": step_ag2, "zbw": step_zbw, "zbo": step_zbo, "xb": step_xb, "yb": step_yb,
        "tx": step_tx, "ty": step_ty, "tg": step_tg, "th": step_th, "ti": step_ti, "tp": step_tp,
    }
    for name, *rest in ORDER:
        table[name](*rest)
    for copy in sent:
        copy.wait_send()
    for copy in outs:
        copy.wait()
    assert count[0] <= SEMS and not pending


SEMS = 384
LIVE = 100


def local(densities, weights, spreads):
    field = (3, CH, 2, 2, 2, 4, 4, 8, 128)
    vmem = pltpu.VMEM
    scratch = [
        vmem((1024, 512), F32), vmem((1024, 512), F32), vmem((CH, 2, 512, 128), F32), vmem((512, 128), F32),
        vmem(field, F32), vmem(field, F32), vmem(field, F32),
        vmem((CH, 16, 64, 128), F32),
        vmem((2, CH, 16, 64, 128), F32),
        vmem((2, CH, 8, 64, 128), F32),
        vmem((2, CH, 8, 64, 128), F32),
        vmem((2, CH, 4, 64, 128), F32),
        vmem((2, CH, 2, 64, 128), F32),
        vmem((CH, 8, 64, 128), F32),
        vmem((CH, 8, 64, 128), F32),
        vmem((2, 2, 2, 4, 4, 8, 128), F32),
        vmem((2, 4, 2, 2, 4, 4, 8, 128), F32),
        vmem((1024, 512), BF), vmem((1024, 512), BF),
        vmem((1024, 256), BF), vmem((1024, 256), BF),
        vmem((512, 512), BF), vmem((512, 512), BF), vmem((512, 512), BF), vmem((512, 512), BF),
        vmem((64, 192), BF),
        vmem((7, 8, 128), F32),
        pltpu.SemaphoreType.DMA((10,)), pltpu.SemaphoreType.DMA((LIVE,)), pltpu.SemaphoreType.DMA((SEMS,)),
    ]
    whole = pl.BlockSpec(memory_space=pl.ANY)
    smem = pl.BlockSpec(memory_space=pltpu.SMEM)
    bary, scale_w = pl.pallas_call(
        body,
        out_shape=[
            jax.ShapeDtypeStruct((8, 2, 64, 512), F32),
            jax.ShapeDtypeStruct((1024, 512), F32),
        ],
        in_specs=[whole, smem, smem],
        out_specs=[whole, whole],
        scratch_shapes=scratch,
        compiler_params=pltpu.CompilerParams(
            collective_id=0, has_side_effects=True, vmem_limit_bytes=61 * 1024 * 1024
        ),
        name="sinkhorn",
    )(densities.reshape(1024, 512), weights, spreads)
    return bary.reshape(2, 512, 512), scale_w.reshape(1, 2, 512, 512)


def solution(mesh):
    return jax.shard_map(
        local,
        mesh=mesh,
        in_specs=(P("dens", "sp", None, None), P("dens"), P()),
        out_specs=(P("sp", None, None), P("dens", "sp", None, None)),
        check_vma=False,
    )
```

```python
import itertools
import math

import jax
import jax.numpy as jnp
from jax import lax
from jax.experimental import pallas as pl
from jax.experimental.pallas import tpu as pltpu
from jax.sharding import PartitionSpec as P

MESH = pl.DeviceIdType.MESH
BF = jnp.bfloat16
F32 = jnp.float32

NXD, NYD, NZD, NHD = 4, 4, 2, 4
CH = 4
SIZE = {"x": NXD, "y": NYD, "z": NZD}
AXES = (
    ((("x", "yz"), ("x", "yz")), (("x", "yz"), ("yz", "x")), (("yz", "x"), ("x", "yz")), (("x", "yz"), ("x", "yz"))),
    ((("x", "yz"), ("x", "yz")), (("x", "yz"), ("x", "yz")), (("x", "yz"), ("yz", "x")), (("x", "yz"), ("yz", "x"))),
    ((("yz", "x"), ("yz", "x")), (("yz", "x"), ("x", "yz")), (("yz", "x"), ("x", "yz")), (("yz", "x"), ("yz", "x"))),
)


ORDER = (
    ("conv", 0, 0), ("conv", 0, 1), ("adv", 0, 0, 0, 0), ("adv", 0, 0, 1, 1), ("adv", 0, 0, 0, 1), ("adv", 0, 0, 2, 0),
    ("adv", 0, 0, 1, 0), ("zo", 0, 0), ("adv", 0, 0, 2, 1), ("zw", 0, 0), ("cs", 0, 0), ("adv", 0, 0, 3, 0), ("zo", 0, 1),
    ("adv", 0, 0, 3, 1), ("zw", 0, 2), ("rs1", 0, 0), ("zw", 0, 1), ("zo", 0, 3), ("cs", 0, 1), ("zo", 0, 2), ("zw", 0, 3),
    ("rs2", 0, 0), ("cs", 0, 3), ("cs", 0, 2), ("rs1", 0, 1), ("ag1", 0, 0), ("rs1", 0, 3), ("rs1", 0, 2), ("rs2", 0, 1),
    ("ag2", 0, 0), ("zbw", 0, 0), ("rs2", 0, 3), ("rs2", 0, 2), ("zbo", 0, 0), ("ag1", 0, 1), ("ag1", 0, 3), ("adv", 1, 0, 0, 1),
    ("ag1", 0, 2), ("adv", 1, 0, 0, 0), ("ag2", 0, 1), ("zbw", 0, 1), ("ag2", 0, 3), ("zbw", 0, 3), ("zbo", 0, 1), ("ag2", 0, 2),
    ("zbw", 0, 2), ("zbo", 0, 3), ("adv", 1, 0, 1, 1), ("zbo", 0, 2), ("adv", 1, 0, 3, 1), ("adv", 1, 0, 1, 0),
    ("adv", 1, 0, 2, 1), ("adv", 1, 0, 3, 0), ("adv", 1, 0, 2, 0), ("xb", 0), ("ya",), ("xb", 1), ("yb",), ("conv", 2, 0), ("conv", 2, 1),
    ("adv", 2, 0, 0, 0), ("adv", 2, 0, 1, 1), ("adv", 2, 0, 0, 1), ("adv", 2, 0, 2, 1), ("adv", 2, 0, 1, 0), ("zo", 2, 0),
    ("adv", 2, 0, 2, 0), ("zw", 2, 0), ("cs", 2, 0), ("adv", 2, 0, 3, 0), ("zo", 2, 1), ("adv", 2, 0, 3, 1), ("zo", 2, 2),
    ("rs1", 2, 0), ("zw", 2, 1), ("zo", 2, 3), ("cs", 2, 1), ("zw", 2, 2), ("zw", 2, 3), ("cs", 2, 2), ("rs2", 2, 0),
    ("cs", 2, 3), ("rs1", 2, 1), ("rs1", 2, 2), ("rs1", 2, 3), ("rs2", 2, 1), ("tx", 0), ("rs2", 2, 2), ("rs2", 2, 3), ("tx", 1),
    ("ty", 0), ("ty", 1), ("tg", 0), ("tg", 1), ("th", 0), ("th", 1), ("ti", 0), ("ti", 1), ("tp", 0), ("tp", 1),
)


def split(x):
    hi = x.astype(BF)
    return hi, (x - hi.astype(F32)).astype(BF)


def dot(a, b):
    return jnp.dot(a, b, preferred_element_type=F32)


def body(
    dens_hbm, wt_ref, spread_ref, bary_hbm, w_hbm,
    dens_ref, w_ref, bary_ref, inv_x, b0, b1, b2, d_ref, t_ref, cb_ref, u_ref, r1_ref, r2_ref, bar_ref, oth_ref,
    share_ref, gath_ref, whi, wlo, thi, tlo, gxh, gxl, gyh, gyl, gz3, wts, io_sem, send_sem, recv_sem,
):
    dens = lax.axis_index("dens")
    sp = lax.axis_index("sp")
    zh, core = dens // 2, lax.rem(dens, 2)
    me = {"y": sp // 8, "z": lax.rem(sp // 4, 2), "x": lax.rem(sp, 4)}

    def device(h=zh, k=core, **at):
        at = {**me, **at}
        return {"dens": h * 2 + k, "sp": (at["y"] * 2 + at["z"]) * 4 + at["x"]}

    def around(axis, k):
        return lax.rem(me[axis] + k, SIZE[axis])

    right, left = lax.rem(zh + 1, 4), lax.rem(zh + 3, 4)
    far = lax.rem(zh + 2, 4)
    zl = me["z"]
    eff = lax.rem(zl + zh, 2)
    one = device(h=lax.rem(zh + 3 + 2 * zl, 4), z=1 - zl)
    two = device(h=lax.rem(zh + 1 + 2 * zl, 4), z=1 - zl)
    gray = lax.rem(zh + zh // 2, 2)
    bit_one = (zh // 2) * (1 - eff) + gray * eff
    bit_two = gray * (1 - eff) + (zh // 2) * eff
    quarter = bit_one * 2 + bit_two
    peers = [device(**{axis: around(axis, k)}) for axis in "xyz" for k in range(1, SIZE[axis])]
    peers += [device(y=around("y", k), z=around("z", 1)) for k in range(1, NYD)]
    peers += [device(k=1 - core), device(h=right), device(h=left), device(h=far), one, two]

    barrier = pltpu.get_barrier_semaphore()
    for peer in peers:
        pl.semaphore_signal(barrier, 1, device_id=peer, device_id_type=MESH)

    fetch = pltpu.make_async_copy(dens_hbm, dens_ref, io_sem.at[0])
    fetch.start()
    root = math.sqrt(math.pi)

    def gauss(i, j, s):
        diff = (i - j).astype(F32) * (1.0 / s)
        return jnp.exp(-diff * diff) * (1.0 / (s * jnp.float32(root)))

    def wide(hi_ref, lo_ref, s):
        def tile(m, total):
            at = pl.multiple_of(m * 64, 64)
            i = lax.broadcasted_iota(jnp.int32, (64, 512), 0) + at
            j = lax.broadcasted_iota(jnp.int32, (64, 512), 1)
            g = gauss(i, j, s)
            hi, lo = split(g)
            hi_ref[pl.ds(at, 64), :] = hi
            lo_ref[pl.ds(at, 64), :] = lo
            if hi_ref is gxh:
                inv_x[pl.ds(at, 64), :] = jnp.broadcast_to(1.0 / jnp.sum(g, axis=1, keepdims=True), (64, 128))
                return total
            return total + jnp.sum(g, axis=0, keepdims=True)
        return lax.fori_loop(0, 8, tile, jnp.zeros((1, 512), F32))

    sum_y = wide(gyh, gyl, spread_ref[2])
    wide(gxh, gxl, spread_ref[1])

    def plane(q):
        return ((q >> 2) & 3) * 16 + (q >> 5) * 8 + (q & 3) * 2 + ((q >> 4) & 1)

    i = lax.broadcasted_iota(jnp.int32, (64, 192), 0)
    j = lax.broadcasted_iota(jnp.int32, (64, 192), 1)
    hi, lo = split(gauss(plane(i), plane(j & 63), spread_ref[0]))
    gz3[...] = jnp.where(j < 128, hi.astype(F32), lo.astype(F32)).astype(BF)

    planes = sp * 2 + lax.broadcasted_iota(jnp.int32, (8, 128), 0)
    others = lax.broadcasted_iota(jnp.int32, (8, 128), 1)
    near = jnp.where(others < 64, gauss(planes, others, spread_ref[0]), 0.0)
    sum_z = jnp.sum(near, axis=1, keepdims=True)

    fetch.wait()
    for p in range(2):
        inv_y = 1.0 / (sum_y * sum_z[p : p + 1, :])

        def first(m, carry):
            rows = pl.ds(pl.multiple_of(p * 512 + m * 64, 64), 64)
            inv = inv_x[pl.ds(pl.multiple_of(m * 64, 64), 64), :]
            hi, lo = split(dens_ref[rows, :] * jnp.concatenate([inv] * 4, axis=1) * inv_y)
            whi[rows, :] = hi
            wlo[rows, :] = lo
            return carry
        lax.fori_loop(0, 8, first, 0)

    pl.semaphore_wait(barrier, len(peers))

    sent = []
    outs = []
    count = [0]
    turn = [0]

    def remote(src, dst, to):
        n = count[0]
        count[0] += 1
        if len(sent) >= LIVE:
            sent.pop(0).wait_send()
        turn[0] = (turn[0] + 1) % LIVE
        copy = pltpu.make_async_remote_copy(
            src, dst, send_sem.at[turn[0]], recv_sem.at[n], device_id=to, device_id_type=MESH
        )
        copy.start()
        sent.append(copy)
        return copy.wait_recv

    def local(src, dst):
        n = count[0]
        count[0] += 1
        copy = pltpu.make_async_copy(src, dst, recv_sem.at[n])
        copy.start()
        return copy.wait

    pending = {}

    def finish(*key):
        for wait in pending.pop(key):
            wait()

    own_rows = pl.ds(pl.multiple_of(core * 8, 8), 8)
    other_rows = pl.ds(pl.multiple_of((1 - core) * 8, 8), 8)

    def slot(ref, lead, at, rows):
        at = tuple(at.get(axis, slice(None)) for axis in "zpyx")
        return ref.at[(*lead, *at) if rows is None else (*lead, *at, rows)]

    def swap(src, s_lead, dst, d_lead, axes, rows, forward):
        waits = []
        for ks in itertools.product(*(range(SIZE[axis]) for axis in axes)):
            to = {axis: around(axis, k) for axis, k in zip(axes, ks)}
            take, put = dict(to), {axis: me[axis] for axis in axes}
            if "z" in axes:
                if forward:
                    take["z"] = lax.rem(eff + ks[axes.index("z")], 2)
                else:
                    put["z"] = eff
            pair = slot(src, s_lead, take, rows), slot(dst, d_lead, put, rows)
            waits.append(remote(*pair, device(**to)) if any(ks) else local(*pair))
        return waits

    bufs = (b0, b1, b2)

    def start(a, j, c, u):
        half = core if u else 1 - core
        pending["a2a", a, j, c, u] = swap(
            bufs[a], (j, c, half), bufs[a], (j + 1, c, half), AXES[a][c][u][j], None, a != 1
        )

    wts[0] = jnp.full((8, 128), wt_ref[0], F32)
    pending["wc",] = [remote(wts.at[0], wts.at[1], device(k=1 - core))]

    def weights():
        finish("wc")
        wts[2] = wts[0] + wts[1]
        pending["wh",] = [
            remote(wts.at[2], wts.at[2 + k], device(h=lax.rem(zh + k, 4))) for k in range(1, 4)
        ]

    def total_weight():
        finish("wh")
        wts[6] = 1.0 / (wts[2] + wts[3] + (wts[4] + wts[5]))

    def step_adv(a, j, c, u):
        finish("a2a", a, j, c, u)
        start(a, j + 1, c, u)

    def step_conv(a, h):
        cols = slice(h * 256, h * 256 + 256)

        def along_y(m, carry):
            rows = pl.ds(pl.multiple_of(m * 256, 256), 256)
            x = dot(whi[rows, :], gyh[:, cols]) + (dot(wlo[rows, :], gyh[:, cols]) + dot(whi[rows, :], gyl[:, cols]))
            hi, lo = split(x)
            thi[rows, :] = hi
            tlo[rows, :] = lo
            return carry
        lax.fori_loop(0, 4, along_y, 0)

        for p in range(2):
            def along_x(m, carry):
                rows = pl.ds(pl.multiple_of(m * 128, 128), 128)
                k = slice(p * 512, p * 512 + 512)
                x = dot(gxh[rows, :], thi[k, :]) + (dot(gxl[rows, :], thi[k, :]) + dot(gxh[rows, :], tlo[k, :]))
                for e in range(2):
                    block = x[:, e * 128 : e * 128 + 128].reshape(2, 4, 2, 8, 128)
                    for half in range(2):
                        bufs[a][0, 2 * h + e, half, :, p, m] = block[:, :, half]
                return carry
            lax.fori_loop(0, 4, along_x, 0)
        for e in range(2):
            start(a, 0, 2 * h + e, 0)
            start(a, 0, 2 * h + e, 1)
        if a == 0 and h == 1:
            weights()

    def columns(x):
        hi, lo = split(x)
        return dot(gz3[...], jnp.concatenate([hi, lo, hi], axis=0))

    def convolved(a, c, half):
        flat = bufs[a].at[2, c, half].reshape(512, 128)
        weight = wt_ref[0]

        def pair(n, carry):
            r = half * 8 + n * 2
            x = jnp.concatenate([flat[pl.ds(n * 2 + e, 64, stride=8), :] for e in range(2)], axis=1)
            y = columns(x)
            for e in range(2):
                part = y[:, e * 128 : e * 128 + 128]
                if a == 0:
                    d_ref[c, r + e] = part
                else:
                    part = d_ref[c, r + e] * part
                t_ref[a // 2, c, r + e] = weight * jnp.log(part)
            return carry
        lax.fori_loop(0, 4, pair, 0)

    def step_zo(a, c):
        ph = a // 2
        finish("a2a", a, 1, c, 0)
        convolved(a, c, 1 - core)
        pending["cs", ph, c] = [remote(t_ref.at[ph, c, other_rows], cb_ref.at[ph, c], device(k=1 - core))]

    def step_zw(a, c):
        finish("a2a", a, 1, c, 1)
        convolved(a, c, core)

    mine = pl.ds(quarter * 2, 2)
    given = pl.ds(bit_one * 4 + (1 - bit_two) * 2, 2)
    half_mine = pl.ds(bit_one * 4, 4)
    half_given = pl.ds((1 - bit_one) * 4, 4)

    def step_cs(a, c):
        ph = a // 2
        finish("cs", ph, c)
        u_ref[ph, c] = t_ref[ph, c, own_rows] + cb_ref[ph, c]
        pending["rs1", ph, c] = [remote(u_ref.at[ph, c, half_given], r1_ref.at[ph, c], one)]

    def step_rs1(a, c):
        ph = a // 2
        finish("rs1", ph, c)
        u_ref[ph, c, half_mine] += r1_ref[ph, c]
        pending["rs2", ph, c] = [remote(u_ref.at[ph, c, given], r2_ref.at[ph, c], two)]

    def step_rs2(a, c):
        ph = a // 2
        if ("wh",) in pending:
            total_weight()
        finish("rs2", ph, c)
        total = u_ref[ph, c, mine] + r2_ref[ph, c]
        mean = jnp.exp(total * wts[6, 0:1, 0:1].reshape(1, 1, 1))
        if a == 0:
            bar_ref[c, mine] = mean
            here = bar_ref.at[c, mine]
            pending["ag1", c] = [remote(here, here, two)]
        else:
            flat = share_ref.at[0].reshape(512, 128)
            for e in range(2):
                flat[pl.ds(c * 2 + e, 64, stride=8), :] = mean[e]

    def step_ag1(a, c):
        finish("ag1", c)
        here = bar_ref.at[c, half_mine]
        pending["ag2", c] = [remote(here, here, one)]

    def step_ag2(a, c):
        finish("ag2", c)
        pending["cg", c] = [remote(bar_ref.at[c], oth_ref.at[c], device(k=1 - core))]

    def scaled(src, c, half):
        flat = b1.at[0, c, half].reshape(512, 128)

        def pair(n, carry):
            r = half * 8 + n * 2
            parts = []
            for e in range(2):
                v = src[c, n * 2 + e] / d_ref[c, r + e]
                d_ref[c, r + e] = v
                parts.append(v)
            y = columns(jnp.concatenate(parts, axis=1))
            for e in range(2):
                flat[pl.ds(n * 2 + e, 64, stride=8), :] = y[:, e * 128 : e * 128 + 128]
            return carry
        lax.fori_loop(0, 4, pair, 0)

    def step_zbw(a, c):
        scaled(bar_ref, c, core)
        start(1, 0, c, 1)

    def step_zbo(a, c):
        finish("cg", c)
        scaled(oth_ref, c, 1 - core)
        start(1, 0, c, 0)

    def step_xb(h):
        for e in range(2):
            finish("a2a", 1, 1, 2 * h + e, 0)
            finish("a2a", 1, 1, 2 * h + e, 1)
        cols = slice(h * 256, h * 256 + 256)
        for p in range(2):
            def block(c, k):
                halves = [b1[2, c, half, k % 2, p, k // 2][:, None] for half in range(2)]
                return jnp.concatenate(halves, axis=1).reshape(64, 128)

            x = jnp.concatenate(
                [jnp.concatenate([block(2 * h + e, k) for k in range(8)], axis=0) for e in range(2)], axis=1
            )
            hi, lo = split(x)
            thi[p * 512 : p * 512 + 512, :] = hi
            tlo[p * 512 : p * 512 + 512, :] = lo

            def along_x(m, carry):
                rows = pl.ds(pl.multiple_of(m * 128, 128), 128)
                to = pl.ds(pl.multiple_of(p * 512 + m * 128, 128), 128)
                k = slice(p * 512, p * 512 + 512)
                x = dot(gxh[rows, :], thi[k, :]) + (dot(gxl[rows, :], thi[k, :]) + dot(gxh[rows, :], tlo[k, :]))
                hi, lo = split(x)
                whi[to, cols] = hi
                wlo[to, cols] = lo
                return carry
            lax.fori_loop(0, 4, along_x, 0)

    def over_lanes(rows, cols):
        a_hi, a_lo = whi[rows, cols], wlo[rows, cols]
        return dot(a_hi, gyh[cols, :]) + (dot(a_lo, gyh[cols, :]) + dot(a_hi, gyl[cols, :]))

    def step_ya():
        def along_y(m, carry):
            rows = pl.ds(pl.multiple_of(m * 128, 128), 128)
            w_ref[rows, :] = over_lanes(rows, slice(0, 256))
            return carry
        lax.fori_loop(0, 8, along_y, 0)

    def step_yb():
        def along_y(m, carry):
            rows = pl.ds(pl.multiple_of(m * 128, 128), 128)
            w = dens_ref[rows, :] / (w_ref[rows, :] + over_lanes(rows, slice(256, 512)))
            w_ref[rows, :] = w
            hi, lo = split(w)
            whi[rows, :] = hi
            wlo[rows, :] = lo
            return carry
        lax.fori_loop(0, 8, along_y, 0)
        copy = pltpu.make_async_copy(w_ref, w_hbm, io_sem.at[1])
        copy.start()
        outs.append(copy)

    def part(ref, h):
        return ref.at[..., pl.ds(h * 4, 4), :]

    def step_tx(h):
        pending["tail", h] = swap(share_ref, (0,), share_ref, (1,), "x", pl.ds(h * 4, 4), False)

    def step_ty(h):
        finish("tail", h)
        pending["tail", h] = swap(share_ref, (1,), gath_ref, (core, zh), "yz", pl.ds(h * 4, 4), False)

    def both(to_right, to_left):
        return [remote(to_right, to_right, device(h=right)), remote(to_left, to_left, device(h=left))]

    def across(h, *at):
        here = part(gath_ref.at[(core,) + at], h)
        pending["over", h].append(remote(here, here, device(k=1 - core)))

    def step_tg(h):
        finish("tail", h)
        here = part(gath_ref.at[core, zh], h)
        pending["tail", h] = both(here, here)
        pending["over", h] = []
        across(h, zh)

    def step_th(h):
        finish("tail", h)
        pending["tail", h] = both(part(gath_ref.at[core, left, 0], h), part(gath_ref.at[core, right, 1], h))
        across(h, left)
        across(h, right)

    def step_ti(h):
        finish("tail", h)
        across(h, far)

    def step_tp(h):
        def place(k):
            for h_from in range(NHD):
                for z in range(2):
                    src = gath_ref.at[k, h_from, z].reshape(256, 128)
                    bits = h_from // 2, (h_from + h_from // 2) % 2
                    row = bits[z] * 4 + bits[1 - z] * 2
                    for c in (2 * h, 2 * h + 1):
                        dst = bary_ref.at[c, z]
                        for e in range(2):
                            dst[pl.ds(k * 8 + row + e, 32, stride=16), :] = src[pl.ds(c * 2 + e, 32, stride=8), :]

        place(core)
        finish("over", h)
        place(1 - core)
        for c in (2 * h, 2 * h + 1):
            for z in range(2):
                copy = pltpu.make_async_copy(
                    bary_ref.at[c, z].reshape(8, 64, 128), bary_hbm.at[:, z, :, pl.ds(c * 128, 128)], io_sem.at[2 + 2 * c + z]
                )
                copy.start()
                outs.append(copy)

    table = {
        "conv": step_conv, "adv": step_adv, "zo": step_zo, "zw": step_zw, "cs": step_cs, "rs1": step_rs1, "rs2": step_rs2,
        "ag1": step_ag1, "ag2": step_ag2, "zbw": step_zbw, "zbo": step_zbo, "xb": step_xb, "ya": step_ya, "yb": step_yb,
        "tx": step_tx, "ty": step_ty, "tg": step_tg, "th": step_th, "ti": step_ti, "tp": step_tp,
    }
    for name, *rest in ORDER:
        table[name](*rest)
    for copy in sent:
        copy.wait_send()
    for copy in outs:
        copy.wait()
    assert count[0] <= SEMS and not pending


SEMS = 384
LIVE = 100


def local(densities, weights, spreads):
    field = (3, CH, 2, 2, 2, 4, 4, 8, 128)
    vmem = pltpu.VMEM
    scratch = [
        vmem((1024, 512), F32), vmem((1024, 512), F32), vmem((CH, 2, 512, 128), F32), vmem((512, 128), F32),
        vmem(field, F32), vmem(field, F32), vmem(field, F32),
        vmem((CH, 16, 64, 128), F32),
        vmem((2, CH, 16, 64, 128), F32),
        vmem((2, CH, 8, 64, 128), F32),
        vmem((2, CH, 8, 64, 128), F32),
        vmem((2, CH, 4, 64, 128), F32),
        vmem((2, CH, 2, 64, 128), F32),
        vmem((CH, 8, 64, 128), F32),
        vmem((CH, 8, 64, 128), F32),
        vmem((2, 2, 2, 4, 4, 8, 128), F32),
        vmem((2, 4, 2, 2, 4, 4, 8, 128), F32),
        vmem((1024, 512), BF), vmem((1024, 512), BF),
        vmem((1024, 256), BF), vmem((1024, 256), BF),
        vmem((512, 512), BF), vmem((512, 512), BF), vmem((512, 512), BF), vmem((512, 512), BF),
        vmem((64, 192), BF),
        vmem((7, 8, 128), F32),
        pltpu.SemaphoreType.DMA((10,)), pltpu.SemaphoreType.DMA((LIVE,)), pltpu.SemaphoreType.DMA((SEMS,)),
    ]
    whole = pl.BlockSpec(memory_space=pl.ANY)
    smem = pl.BlockSpec(memory_space=pltpu.SMEM)
    bary, scale_w = pl.pallas_call(
        body,
        out_shape=[
            jax.ShapeDtypeStruct((8, 2, 64, 512), F32),
            jax.ShapeDtypeStruct((1024, 512), F32),
        ],
        in_specs=[whole, smem, smem],
        out_specs=[whole, whole],
        scratch_shapes=scratch,
        compiler_params=pltpu.CompilerParams(
            collective_id=0, has_side_effects=True, vmem_limit_bytes=61 * 1024 * 1024
        ),
        name="sinkhorn",
    )(densities.reshape(1024, 512), weights, spreads)
    return bary.reshape(2, 512, 512), scale_w.reshape(1, 2, 512, 512)


def solution(mesh):
    return jax.shard_map(
        local,
        mesh=mesh,
        in_specs=(P("dens", "sp", None, None), P("dens"), P()),
        out_specs=(P("sp", None, None), P("dens", "sp", None, None)),
        check_vma=False,
    )
```

```python
import itertools
import math

import jax
import jax.numpy as jnp
from jax import lax
from jax.experimental import pallas as pl
from jax.experimental.pallas import tpu as pltpu
from jax.sharding import PartitionSpec as P

MESH = pl.DeviceIdType.MESH
BF = jnp.bfloat16
F32 = jnp.float32

NXD, NYD, NZD, NHD = 4, 4, 2, 4
CH = 4
SIZE = {"x": NXD, "y": NYD, "z": NZD}
AXES = (
    ((("x", "yz"), ("yz", "x")), (("yz", "x"), ("x", "yz")), (("x", "yz"), ("yz", "x")), (("yz", "x"), ("x", "yz"))),
    ((("x", "yz"), ("yz", "x")), (("yz", "x"), ("x", "yz")), (("x", "yz"), ("yz", "x")), (("yz", "x"), ("x", "yz"))),
    ((("x", "yz"), ("yz", "x")), (("yz", "x"), ("x", "yz")), (("x", "yz"), ("yz", "x")), (("yz", "x"), ("x", "yz"))),
)


ORDER = (
    ("conv", 0, 0), ("conv", 0, 1), ("adv", 0, 0, 0, 0), ("adv", 0, 0, 0, 1), ("adv", 0, 0, 1, 0), ("adv", 0, 0, 1, 1),
    ("adv", 0, 0, 2, 0), ("adv", 0, 0, 2, 1), ("adv", 0, 0, 3, 0), ("adv", 0, 0, 3, 1), ("zo", 0, 0), ("zw", 0, 0), ("zo", 0, 1),
    ("zw", 0, 1), ("cs", 0, 0), ("zo", 0, 2), ("zw", 0, 2), ("cs", 0, 1), ("zo", 0, 3), ("zw", 0, 3), ("cs", 0, 2), ("rs1", 0, 0),
    ("cs", 0, 3), ("rs1", 0, 1), ("rs1", 0, 2), ("rs2", 0, 0), ("rs1", 0, 3), ("rs2", 0, 1), ("rs2", 0, 2), ("ag1", 0, 0),
    ("rs2", 0, 3), ("ag1", 0, 1), ("ag1", 0, 2), ("ag2", 0, 0), ("zbw", 0, 0), ("ag1", 0, 3), ("zbo", 0, 0), ("ag2", 0, 1),
    ("zbw", 0, 1), ("adv", 1, 0, 0, 1), ("ag2", 0, 2), ("zbw", 0, 2), ("zbo", 0, 1), ("ag2", 0, 3), ("zbw", 0, 3), ("zbo", 0, 2),
    ("adv", 1, 0, 0, 0), ("adv", 1, 0, 1, 1), ("zbo", 0, 3), ("adv", 1, 0, 2, 1), ("adv", 1, 0, 1, 0), ("adv", 1, 0, 3, 1),
    ("adv", 1, 0, 2, 0), ("adv", 1, 0, 3, 0), ("xb", 0), ("ya",), ("xb", 1), ("yb",), ("conv", 2, 0), ("conv", 2, 1), ("adv", 2, 0, 0, 0),
    ("adv", 2, 0, 0, 1), ("adv", 2, 0, 1, 0), ("adv", 2, 0, 1, 1), ("adv", 2, 0, 2, 0), ("adv", 2, 0, 2, 1), ("adv", 2, 0, 3, 0),
    ("adv", 2, 0, 3, 1), ("zo", 2, 0), ("zw", 2, 0), ("zo", 2, 1), ("zw", 2, 1), ("cs", 2, 0), ("zo", 2, 2), ("zw", 2, 2),
    ("cs", 2, 1), ("zo", 2, 3), ("zw", 2, 3), ("cs", 2, 2), ("rs1", 2, 0), ("cs", 2, 3), ("rs1", 2, 1), ("rs1", 2, 2),
    ("rs2", 2, 0), ("rs1", 2, 3), ("rs2", 2, 1), ("tx", 0), ("rs2", 2, 2), ("rs2", 2, 3), ("tx", 1), ("ty", 0), ("ty", 1),
    ("tg", 0), ("tg", 1), ("th", 0), ("th", 1), ("ti", 0), ("ti", 1), ("tp", 0), ("tp", 1),
)


def split(x):
    hi = x.astype(BF)
    return hi, (x - hi.astype(F32)).astype(BF)


def dot(a, b):
    return jnp.dot(a, b, preferred_element_type=F32)


def body(
    dens_hbm, wt_ref, spread_ref, bary_hbm, w_hbm,
    dens_ref, w_ref, bary_ref, inv_x, b0, b1, b2, d_ref, t_ref, cb_ref, u_ref, r1_ref, r2_ref, bar_ref, oth_ref,
    share_ref, gath_ref, whi, wlo, thi, tlo, gxh, gxl, gyh, gyl, gz3, wts, io_sem, send_sem, recv_sem,
):
    dens = lax.axis_index("dens")
    sp = lax.axis_index("sp")
    zh, core = dens // 2, lax.rem(dens, 2)
    me = {"y": sp // 8, "z": lax.rem(sp // 4, 2), "x": lax.rem(sp, 4)}

    def device(h=zh, k=core, **at):
        at = {**me, **at}
        return {"dens": h * 2 + k, "sp": (at["y"] * 2 + at["z"]) * 4 + at["x"]}

    def around(axis, k):
        return lax.rem(me[axis] + k, SIZE[axis])

    right, left = lax.rem(zh + 1, 4), lax.rem(zh + 3, 4)
    far = lax.rem(zh + 2, 4)
    zl = me["z"]
    eff = lax.rem(zl + zh, 2)
    one = device(h=lax.rem(zh + 3 + 2 * zl, 4), z=1 - zl)
    two = device(h=lax.rem(zh + 1 + 2 * zl, 4), z=1 - zl)
    gray = lax.rem(zh + zh // 2, 2)
    bit_one = (zh // 2) * (1 - eff) + gray * eff
    bit_two = gray * (1 - eff) + (zh // 2) * eff
    quarter = bit_one * 2 + bit_two
    peers = [device(**{axis: around(axis, k)}) for axis in "xyz" for k in range(1, SIZE[axis])]
    peers += [device(y=around("y", k), z=around("z", 1)) for k in range(1, NYD)]
    peers += [device(k=1 - core), device(h=right), device(h=left), device(h=far), one, two]

    barrier = pltpu.get_barrier_semaphore()
    for peer in peers:
        pl.semaphore_signal(barrier, 1, device_id=peer, device_id_type=MESH)

    fetch = pltpu.make_async_copy(dens_hbm, dens_ref, io_sem.at[0])
    fetch.start()
    root = math.sqrt(math.pi)

    def gauss(i, j, s):
        diff = (i - j).astype(F32) * (1.0 / s)
        return jnp.exp(-diff * diff) * (1.0 / (s * jnp.float32(root)))

    def wide(hi_ref, lo_ref, s):
        def tile(m, total):
            at = pl.multiple_of(m * 64, 64)
            i = lax.broadcasted_iota(jnp.int32, (64, 512), 0) + at
            j = lax.broadcasted_iota(jnp.int32, (64, 512), 1)
            g = gauss(i, j, s)
            hi, lo = split(g)
            hi_ref[pl.ds(at, 64), :] = hi
            lo_ref[pl.ds(at, 64), :] = lo
            if hi_ref is gxh:
                inv_x[pl.ds(at, 64), :] = jnp.broadcast_to(1.0 / jnp.sum(g, axis=1, keepdims=True), (64, 128))
                return total
            return total + jnp.sum(g, axis=0, keepdims=True)
        return lax.fori_loop(0, 8, tile, jnp.zeros((1, 512), F32))

    sum_y = wide(gyh, gyl, spread_ref[2])
    wide(gxh, gxl, spread_ref[1])

    def plane(q):
        return ((q >> 2) & 3) * 16 + (q >> 5) * 8 + (q & 3) * 2 + ((q >> 4) & 1)

    i = lax.broadcasted_iota(jnp.int32, (64, 192), 0)
    j = lax.broadcasted_iota(jnp.int32, (64, 192), 1)
    hi, lo = split(gauss(plane(i), plane(j & 63), spread_ref[0]))
    gz3[...] = jnp.where(j < 128, hi.astype(F32), lo.astype(F32)).astype(BF)

    planes = sp * 2 + lax.broadcasted_iota(jnp.int32, (8, 128), 0)
    others = lax.broadcasted_iota(jnp.int32, (8, 128), 1)
    near = jnp.where(others < 64, gauss(planes, others, spread_ref[0]), 0.0)
    sum_z = jnp.sum(near, axis=1, keepdims=True)

    fetch.wait()
    for p in range(2):
        inv_y = 1.0 / (sum_y * sum_z[p : p + 1, :])

        def first(m, carry):
            rows = pl.ds(pl.multiple_of(p * 512 + m * 64, 64), 64)
            inv = inv_x[pl.ds(pl.multiple_of(m * 64, 64), 64), :]
            hi, lo = split(dens_ref[rows, :] * jnp.concatenate([inv] * 4, axis=1) * inv_y)
            whi[rows, :] = hi
            wlo[rows, :] = lo
            return carry
        lax.fori_loop(0, 8, first, 0)

    pl.semaphore_wait(barrier, len(peers))

    sent = []
    outs = []
    count = [0]
    turn = [0]

    def remote(src, dst, to):
        n = count[0]
        count[0] += 1
        if len(sent) >= LIVE:
            sent.pop(0).wait_send()
        turn[0] = (turn[0] + 1) % LIVE
        copy = pltpu.make_async_remote_copy(
            src, dst, send_sem.at[turn[0]], recv_sem.at[n], device_id=to, device_id_type=MESH
        )
        copy.start()
        sent.append(copy)
        return copy.wait_recv

    def local(src, dst):
        n = count[0]
        count[0] += 1
        copy = pltpu.make_async_copy(src, dst, recv_sem.at[n])
        copy.start()
        return copy.wait

    pending = {}

    def finish(*key):
        for wait in pending.pop(key):
            wait()

    own_rows = pl.ds(pl.multiple_of(core * 8, 8), 8)
    other_rows = pl.ds(pl.multiple_of((1 - core) * 8, 8), 8)

    def slot(ref, lead, at, rows):
        at = tuple(at.get(axis, slice(None)) for axis in "zpyx")
        return ref.at[(*lead, *at) if rows is None else (*lead, *at, rows)]

    def swap(src, s_lead, dst, d_lead, axes, rows, forward):
        waits = []
        for ks in itertools.product(*(range(SIZE[axis]) for axis in axes)):
            to = {axis: around(axis, k) for axis, k in zip(axes, ks)}
            take, put = dict(to), {axis: me[axis] for axis in axes}
            if "z" in axes:
                if forward:
                    take["z"] = lax.rem(eff + ks[axes.index("z")], 2)
                else:
                    put["z"] = eff
            pair = slot(src, s_lead, take, rows), slot(dst, d_lead, put, rows)
            waits.append(remote(*pair, device(**to)) if any(ks) else local(*pair))
        return waits

    bufs = (b0, b1, b2)

    def start(a, j, c, u):
        half = core if u else 1 - core
        pending["a2a", a, j, c, u] = swap(
            bufs[a], (j, c, half), bufs[a], (j + 1, c, half), AXES[a][c][u][j], None, a != 1
        )

    wts[0] = jnp.full((8, 128), wt_ref[0], F32)
    pending["wc",] = [remote(wts.at[0], wts.at[1], device(k=1 - core))]

    def weights():
        finish("wc")
        wts[2] = wts[0] + wts[1]
        pending["wh",] = [
            remote(wts.at[2], wts.at[2 + k], device(h=lax.rem(zh + k, 4))) for k in range(1, 4)
        ]

    def total_weight():
        finish("wh")
        wts[6] = 1.0 / (wts[2] + wts[3] + (wts[4] + wts[5]))

    def step_adv(a, j, c, u):
        finish("a2a", a, j, c, u)
        start(a, j + 1, c, u)

    def step_conv(a, h):
        cols = slice(h * 256, h * 256 + 256)

        def along_y(m, carry):
            rows = pl.ds(pl.multiple_of(m * 256, 256), 256)
            x = dot(whi[rows, :], gyh[:, cols]) + (dot(wlo[rows, :], gyh[:, cols]) + dot(whi[rows, :], gyl[:, cols]))
            hi, lo = split(x)
            thi[rows, :] = hi
            tlo[rows, :] = lo
            return carry
        lax.fori_loop(0, 4, along_y, 0)

        for p in range(2):
            def along_x(m, carry):
                rows = pl.ds(pl.multiple_of(m * 128, 128), 128)
                k = slice(p * 512, p * 512 + 512)
                x = dot(gxh[rows, :], thi[k, :]) + (dot(gxl[rows, :], thi[k, :]) + dot(gxh[rows, :], tlo[k, :]))
                for e in range(2):
                    block = x[:, e * 128 : e * 128 + 128].reshape(2, 4, 2, 8, 128)
                    for half in range(2):
                        bufs[a][0, 2 * h + e, half, :, p, m] = block[:, :, half]
                return carry
            lax.fori_loop(0, 4, along_x, 0)
        for e in range(2):
            start(a, 0, 2 * h + e, 0)
            start(a, 0, 2 * h + e, 1)
        if a == 0 and h == 1:
            weights()

    def columns(x):
        hi, lo = split(x)
        return dot(gz3[...], jnp.concatenate([hi, lo, hi], axis=0))

    def convolved(a, c, half):
        flat = bufs[a].at[2, c, half].reshape(512, 128)
        weight = wt_ref[0]

        def pair(n, carry):
            r = half * 8 + n * 2
            x = jnp.concatenate([flat[pl.ds(n * 2 + e, 64, stride=8), :] for e in range(2)], axis=1)
            y = columns(x)
            for e in range(2):
                part = y[:, e * 128 : e * 128 + 128]
                if a == 0:
                    d_ref[c, r + e] = part
                else:
                    part = d_ref[c, r + e] * part
                t_ref[a // 2, c, r + e] = weight * jnp.log(part)
            return carry
        lax.fori_loop(0, 4, pair, 0)

    def step_zo(a, c):
        ph = a // 2
        finish("a2a", a, 1, c, 0)
        convolved(a, c, 1 - core)
        pending["cs", ph, c] = [remote(t_ref.at[ph, c, other_rows], cb_ref.at[ph, c], device(k=1 - core))]

    def step_zw(a, c):
        finish("a2a", a, 1, c, 1)
        convolved(a, c, core)

    mine = pl.ds(quarter * 2, 2)
    given = pl.ds(bit_one * 4 + (1 - bit_two) * 2, 2)
    half_mine = pl.ds(bit_one * 4, 4)
    half_given = pl.ds((1 - bit_one) * 4, 4)

    def step_cs(a, c):
        ph = a // 2
        finish("cs", ph, c)
        u_ref[ph, c] = t_ref[ph, c, own_rows] + cb_ref[ph, c]
        pending["rs1", ph, c] = [remote(u_ref.at[ph, c, half_given], r1_ref.at[ph, c], one)]

    def step_rs1(a, c):
        ph = a // 2
        finish("rs1", ph, c)
        u_ref[ph, c, half_mine] += r1_ref[ph, c]
        pending["rs2", ph, c] = [remote(u_ref.at[ph, c, given], r2_ref.at[ph, c], two)]

    def step_rs2(a, c):
        ph = a // 2
        if ("wh",) in pending:
            total_weight()
        finish("rs2", ph, c)
        total = u_ref[ph, c, mine] + r2_ref[ph, c]
        mean = jnp.exp(total * wts[6, 0:1, 0:1].reshape(1, 1, 1))
        if a == 0:
            bar_ref[c, mine] = mean
            here = bar_ref.at[c, mine]
            pending["ag1", c] = [remote(here, here, two)]
        else:
            flat = share_ref.at[0].reshape(512, 128)
            for e in range(2):
                flat[pl.ds(c * 2 + e, 64, stride=8), :] = mean[e]

    def step_ag1(a, c):
        finish("ag1", c)
        here = bar_ref.at[c, half_mine]
        pending["ag2", c] = [remote(here, here, one)]

    def step_ag2(a, c):
        finish("ag2", c)
        pending["cg", c] = [remote(bar_ref.at[c], oth_ref.at[c], device(k=1 - core))]

    def scaled(src, c, half):
        flat = b1.at[0, c, half].reshape(512, 128)

        def pair(n, carry):
            r = half * 8 + n * 2
            parts = []
            for e in range(2):
                v = src[c, n * 2 + e] / d_ref[c, r + e]
                d_ref[c, r + e] = v
                parts.append(v)
            y = columns(jnp.concatenate(parts, axis=1))
            for e in range(2):
                flat[pl.ds(n * 2 + e, 64, stride=8), :] = y[:, e * 128 : e * 128 + 128]
            return carry
        lax.fori_loop(0, 4, pair, 0)

    def step_zbw(a, c):
        scaled(bar_ref, c, core)
        start(1, 0, c, 1)

    def step_zbo(a, c):
        finish("cg", c)
        scaled(oth_ref, c, 1 - core)
        start(1, 0, c, 0)

    def step_xb(h):
        for e in range(2):
            finish("a2a", 1, 1, 2 * h + e, 0)
            finish("a2a", 1, 1, 2 * h + e, 1)
        cols = slice(h * 256, h * 256 + 256)
        for p in range(2):
            def block(c, k):
                halves = [b1[2, c, half, k % 2, p, k // 2][:, None] for half in range(2)]
                return jnp.concatenate(halves, axis=1).reshape(64, 128)

            x = jnp.concatenate(
                [jnp.concatenate([block(2 * h + e, k) for k in range(8)], axis=0) for e in range(2)], axis=1
            )
            hi, lo = split(x)
            thi[p * 512 : p * 512 + 512, :] = hi
            tlo[p * 512 : p * 512 + 512, :] = lo

            def along_x(m, carry):
                rows = pl.ds(pl.multiple_of(m * 128, 128), 128)
                to = pl.ds(pl.multiple_of(p * 512 + m * 128, 128), 128)
                k = slice(p * 512, p * 512 + 512)
                x = dot(gxh[rows, :], thi[k, :]) + (dot(gxl[rows, :], thi[k, :]) + dot(gxh[rows, :], tlo[k, :]))
                hi, lo = split(x)
                whi[to, cols] = hi
                wlo[to, cols] = lo
                return carry
            lax.fori_loop(0, 4, along_x, 0)

    def over_lanes(rows, cols):
        a_hi, a_lo = whi[rows, cols], wlo[rows, cols]
        return dot(a_hi, gyh[cols, :]) + (dot(a_lo, gyh[cols, :]) + dot(a_hi, gyl[cols, :]))

    def step_ya():
        def along_y(m, carry):
            rows = pl.ds(pl.multiple_of(m * 128, 128), 128)
            w_ref[rows, :] = over_lanes(rows, slice(0, 256))
            return carry
        lax.fori_loop(0, 8, along_y, 0)

    def step_yb():
        def along_y(m, carry):
            rows = pl.ds(pl.multiple_of(m * 128, 128), 128)
            w = dens_ref[rows, :] / (w_ref[rows, :] + over_lanes(rows, slice(256, 512)))
            w_ref[rows, :] = w
            hi, lo = split(w)
            whi[rows, :] = hi
            wlo[rows, :] = lo
            return carry
        lax.fori_loop(0, 8, along_y, 0)
        copy = pltpu.make_async_copy(w_ref, w_hbm, io_sem.at[1])
        copy.start()
        outs.append(copy)

    def part(ref, h):
        return ref.at[..., pl.ds(h * 4, 4), :]

    def step_tx(h):
        pending["tail", h] = swap(share_ref, (0,), share_ref, (1,), "x", pl.ds(h * 4, 4), False)

    def step_ty(h):
        finish("tail", h)
        pending["tail", h] = swap(share_ref, (1,), gath_ref, (core, zh), "yz", pl.ds(h * 4, 4), False)

    def both(to_right, to_left):
        return [remote(to_right, to_right, device(h=right)), remote(to_left, to_left, device(h=left))]

    def across(h, *at):
        here = part(gath_ref.at[(core,) + at], h)
        pending["over", h].append(remote(here, here, device(k=1 - core)))

    def step_tg(h):
        finish("tail", h)
        here = part(gath_ref.at[core, zh], h)
        pending["tail", h] = both(here, here)
        pending["over", h] = []
        across(h, zh)

    def step_th(h):
        finish("tail", h)
        pending["tail", h] = both(part(gath_ref.at[core, left, 0], h), part(gath_ref.at[core, right, 1], h))
        across(h, left)
        across(h, right)

    def step_ti(h):
        finish("tail", h)
        across(h, far)

    def step_tp(h):
        def place(k):
            for h_from in range(NHD):
                for z in range(2):
                    src = gath_ref.at[k, h_from, z].reshape(256, 128)
                    bits = h_from // 2, (h_from + h_from // 2) % 2
                    row = bits[z] * 4 + bits[1 - z] * 2
                    for c in (2 * h, 2 * h + 1):
                        dst = bary_ref.at[c, z]
                        for e in range(2):
                            dst[pl.ds(k * 8 + row + e, 32, stride=16), :] = src[pl.ds(c * 2 + e, 32, stride=8), :]

        place(core)
        finish("over", h)
        place(1 - core)
        for c in (2 * h, 2 * h + 1):
            for z in range(2):
                copy = pltpu.make_async_copy(
                    bary_ref.at[c, z].reshape(8, 64, 128), bary_hbm.at[:, z, :, pl.ds(c * 128, 128)], io_sem.at[2 + 2 * c + z]
                )
                copy.start()
                outs.append(copy)

    table = {
        "conv": step_conv, "adv": step_adv, "zo": step_zo, "zw": step_zw, "cs": step_cs, "rs1": step_rs1, "rs2": step_rs2,
        "ag1": step_ag1, "ag2": step_ag2, "zbw": step_zbw, "zbo": step_zbo, "xb": step_xb, "ya": step_ya, "yb": step_yb,
        "tx": step_tx, "ty": step_ty, "tg": step_tg, "th": step_th, "ti": step_ti, "tp": step_tp,
    }
    for name, *rest in ORDER:
        table[name](*rest)
    for copy in sent:
        copy.wait_send()
    for copy in outs:
        copy.wait()
    assert count[0] <= SEMS and not pending


SEMS = 384
LIVE = 100


def local(densities, weights, spreads):
    field = (3, CH, 2, 2, 2, 4, 4, 8, 128)
    vmem = pltpu.VMEM
    scratch = [
        vmem((1024, 512), F32), vmem((1024, 512), F32), vmem((CH, 2, 512, 128), F32), vmem((512, 128), F32),
        vmem(field, F32), vmem(field, F32), vmem(field, F32),
        vmem((CH, 16, 64, 128), F32),
        vmem((2, CH, 16, 64, 128), F32),
        vmem((2, CH, 8, 64, 128), F32),
        vmem((2, CH, 8, 64, 128), F32),
        vmem((2, CH, 4, 64, 128), F32),
        vmem((2, CH, 2, 64, 128), F32),
        vmem((CH, 8, 64, 128), F32),
        vmem((CH, 8, 64, 128), F32),
        vmem((2, 2, 2, 4, 4, 8, 128), F32),
        vmem((2, 4, 2, 2, 4, 4, 8, 128), F32),
        vmem((1024, 512), BF), vmem((1024, 512), BF),
        vmem((1024, 256), BF), vmem((1024, 256), BF),
        vmem((512, 512), BF), vmem((512, 512), BF), vmem((512, 512), BF), vmem((512, 512), BF),
        vmem((64, 192), BF),
        vmem((7, 8, 128), F32),
        pltpu.SemaphoreType.DMA((10,)), pltpu.SemaphoreType.DMA((LIVE,)), pltpu.SemaphoreType.DMA((SEMS,)),
    ]
    whole = pl.BlockSpec(memory_space=pl.ANY)
    smem = pl.BlockSpec(memory_space=pltpu.SMEM)
    bary, scale_w = pl.pallas_call(
        body,
        out_shape=[
            jax.ShapeDtypeStruct((8, 2, 64, 512), F32),
            jax.ShapeDtypeStruct((1024, 512), F32),
        ],
        in_specs=[whole, smem, smem],
        out_specs=[whole, whole],
        scratch_shapes=scratch,
        compiler_params=pltpu.CompilerParams(
            collective_id=0, has_side_effects=True, vmem_limit_bytes=61 * 1024 * 1024
        ),
        name="sinkhorn",
    )(densities.reshape(1024, 512), weights, spreads)
    return bary.reshape(2, 512, 512), scale_w.reshape(1, 2, 512, 512)


def solution(mesh):
    return jax.shard_map(
        local,
        mesh=mesh,
        in_specs=(P("dens", "sp", None, None), P("dens"), P()),
        out_specs=(P("sp", None, None), P("dens", "sp", None, None)),
        check_vma=False,
    )
```

```python
import itertools
import math

import jax
import jax.numpy as jnp
from jax import lax
from jax.experimental import pallas as pl
from jax.experimental.pallas import tpu as pltpu
from jax.sharding import PartitionSpec as P

MESH = pl.DeviceIdType.MESH
BF = jnp.bfloat16
F32 = jnp.float32

NXD, NYD, NZD, NHD = 4, 4, 2, 4
CH = 4
SIZE = {"x": NXD, "y": NYD, "z": NZD}
AXES = (
    ((("x", "yz"), ("x", "yz")), (("x", "yz"), ("yz", "x")), (("yz", "x"), ("x", "yz")), (("x", "yz"), ("x", "yz"))),
    ((("x", "yz"), ("x", "yz")), (("x", "yz"), ("x", "yz")), (("x", "yz"), ("yz", "x")), (("x", "yz"), ("yz", "x"))),
    ((("yz", "x"), ("yz", "x")), (("yz", "x"), ("x", "yz")), (("yz", "x"), ("x", "yz")), (("yz", "x"), ("yz", "x"))),
)


ORDER = (
    ("conv", 0, 0), ("conv", 0, 1), ("adv", 0, 0, 0, 0), ("adv", 0, 0, 1, 1), ("adv", 0, 0, 0, 1), ("adv", 0, 0, 2, 0),
    ("adv", 0, 0, 1, 0), ("zo", 0, 0), ("adv", 0, 0, 2, 1), ("zw", 0, 0), ("adv", 0, 0, 3, 0), ("cs", 0, 0), ("zo", 0, 1),
    ("adv", 0, 0, 3, 1), ("zw", 0, 2), ("zw", 0, 1), ("cs", 0, 1), ("zo", 0, 3), ("rs1", 0, 0), ("zo", 0, 2), ("zw", 0, 3),
    ("cs", 0, 3), ("rs1", 0, 1), ("cs", 0, 2), ("rs2", 0, 0), ("rs1", 0, 3), ("rs2", 0, 1), ("rs1", 0, 2), ("ag1", 0, 0),
    ("rs2", 0, 3), ("ag1", 0, 1), ("rs2", 0, 2), ("ag2", 0, 0), ("zbw", 0, 0), ("ag1", 0, 3), ("ag2", 0, 1), ("zbw", 0, 1),
    ("zbo", 0, 0), ("ag1", 0, 2), ("adv", 1, 0, 0, 1), ("ag2", 0, 3), ("zbw", 0, 3), ("zbo", 0, 1), ("adv", 1, 0, 1, 1),
    ("ag2", 0, 2), ("zbw", 0, 2), ("zbo", 0, 3), ("adv", 1, 0, 0, 0), ("zbo", 0, 2), ("adv", 1, 0, 1, 0), ("adv", 1, 0, 3, 1),
    ("adv", 1, 0, 3, 0), ("adv", 1, 0, 2, 1), ("adv", 1, 0, 2, 0), ("xb", 0), ("ya",), ("xb", 1), ("yb",), ("conv", 2, 0),
    ("conv", 2, 1), ("adv", 2, 0, 0, 0), ("adv", 2, 0, 1, 1), ("adv", 2, 0, 0, 1), ("adv", 2, 0, 2, 1), ("adv", 2, 0, 1, 0),
    ("zo", 2, 0), ("adv", 2, 0, 2, 0), ("zw", 2, 0), ("adv", 2, 0, 3, 0), ("cs", 2, 0), ("zo", 2, 1), ("adv", 2, 0, 3, 1),
    ("zo", 2, 2), ("zw", 2, 1), ("cs", 2, 1), ("zo", 2, 3), ("rs1", 2, 0), ("zw", 2, 2), ("cs", 2, 2), ("zw", 2, 3), ("cs", 2, 3),
    ("rs1", 2, 1), ("rs2", 2, 0), ("rs1", 2, 2), ("rs1", 2, 3), ("rs2", 2, 1), ("tx", 0), ("rs2", 2, 2), ("rs2", 2, 3), ("tx", 1),
    ("ty", 0), ("ty", 1), ("tg", 0), ("tg", 1), ("th", 0), ("th", 1), ("ti", 0), ("ti", 1), ("tp", 0), ("tp", 1),
)


def split(x):
    hi = x.astype(BF)
    return hi, (x - hi.astype(F32)).astype(BF)


def dot(a, b):
    return jnp.dot(a, b, preferred_element_type=F32)


def body(
    dens_hbm, wt_ref, spread_ref, bary_hbm, w_hbm,
    dens_ref, w_ref, bary_ref, inv_x, b0, b1, b2, d_ref, t_ref, cb_ref, u_ref, r1_ref, r2_ref, bar_ref, oth_ref,
    share_ref, gath_ref, whi, wlo, thi, tlo, gxh, gxl, gyh, gyl, gz3, wts, io_sem, send_sem, recv_sem,
):
    dens = lax.axis_index("dens")
    sp = lax.axis_index("sp")
    zh, core = dens // 2, lax.rem(dens, 2)
    me = {"y": sp // 8, "z": lax.rem(sp // 4, 2), "x": lax.rem(sp, 4)}

    def device(h=zh, k=core, **at):
        at = {**me, **at}
        return {"dens": h * 2 + k, "sp": (at["y"] * 2 + at["z"]) * 4 + at["x"]}

    def around(axis, k):
        return lax.rem(me[axis] + k, SIZE[axis])

    right, left = lax.rem(zh + 1, 4), lax.rem(zh + 3, 4)
    far = lax.rem(zh + 2, 4)
    zl = me["z"]
    eff = lax.rem(zl + zh, 2)
    one = device(h=lax.rem(zh + 3 + 2 * zl, 4), z=1 - zl)
    two = device(h=lax.rem(zh + 1 + 2 * zl, 4), z=1 - zl)
    gray = lax.rem(zh + zh // 2, 2)
    bit_one = (zh // 2) * (1 - eff) + gray * eff
    bit_two = gray * (1 - eff) + (zh // 2) * eff
    quarter = bit_one * 2 + bit_two
    peers = [device(**{axis: around(axis, k)}) for axis in "xyz" for k in range(1, SIZE[axis])]
    peers += [device(y=around("y", k), z=around("z", 1)) for k in range(1, NYD)]
    peers += [device(k=1 - core), device(h=right), device(h=left), device(h=far), one, two]

    barrier = pltpu.get_barrier_semaphore()
    for peer in peers:
        pl.semaphore_signal(barrier, 1, device_id=peer, device_id_type=MESH)

    fetch = pltpu.make_async_copy(dens_hbm, dens_ref, io_sem.at[0])
    fetch.start()
    root = math.sqrt(math.pi)

    def gauss(i, j, s):
        diff = (i - j).astype(F32) * (1.0 / s)
        return jnp.exp(-diff * diff) * (1.0 / (s * jnp.float32(root)))

    def wide(hi_ref, lo_ref, s):
        def tile(m, total):
            at = pl.multiple_of(m * 64, 64)
            i = lax.broadcasted_iota(jnp.int32, (64, 512), 0) + at
            j = lax.broadcasted_iota(jnp.int32, (64, 512), 1)
            g = gauss(i, j, s)
            hi, lo = split(g)
            hi_ref[pl.ds(at, 64), :] = hi
            lo_ref[pl.ds(at, 64), :] = lo
            if hi_ref is gxh:
                inv_x[pl.ds(at, 64), :] = jnp.broadcast_to(1.0 / jnp.sum(g, axis=1, keepdims=True), (64, 128))
                return total
            return total + jnp.sum(g, axis=0, keepdims=True)
        return lax.fori_loop(0, 8, tile, jnp.zeros((1, 512), F32))

    sum_y = wide(gyh, gyl, spread_ref[2])
    wide(gxh, gxl, spread_ref[1])

    def plane(q):
        return ((q >> 2) & 3) * 16 + (q >> 5) * 8 + (q & 3) * 2 + ((q >> 4) & 1)

    i = lax.broadcasted_iota(jnp.int32, (64, 192), 0)
    j = lax.broadcasted_iota(jnp.int32, (64, 192), 1)
    hi, lo = split(gauss(plane(i), plane(j & 63), spread_ref[0]))
    gz3[...] = jnp.where(j < 128, hi.astype(F32), lo.astype(F32)).astype(BF)

    planes = sp * 2 + lax.broadcasted_iota(jnp.int32, (8, 128), 0)
    others = lax.broadcasted_iota(jnp.int32, (8, 128), 1)
    near = jnp.where(others < 64, gauss(planes, others, spread_ref[0]), 0.0)
    sum_z = jnp.sum(near, axis=1, keepdims=True)

    fetch.wait()
    for p in range(2):
        inv_y = 1.0 / (sum_y * sum_z[p : p + 1, :])

        def first(m, carry):
            rows = pl.ds(pl.multiple_of(p * 512 + m * 64, 64), 64)
            inv = inv_x[pl.ds(pl.multiple_of(m * 64, 64), 64), :]
            hi, lo = split(dens_ref[rows, :] * jnp.concatenate([inv] * 4, axis=1) * inv_y)
            whi[rows, :] = hi
            wlo[rows, :] = lo
            return carry
        lax.fori_loop(0, 8, first, 0)

    pl.semaphore_wait(barrier, len(peers))

    sent = []
    outs = []
    count = [0]
    turn = [0]

    def remote(src, dst, to):
        n = count[0]
        count[0] += 1
        if len(sent) >= LIVE:
            sent.pop(0).wait_send()
        turn[0] = (turn[0] + 1) % LIVE
        copy = pltpu.make_async_remote_copy(
            src, dst, send_sem.at[turn[0]], recv_sem.at[n], device_id=to, device_id_type=MESH
        )
        copy.start()
        sent.append(copy)
        return copy.wait_recv

    def local(src, dst):
        n = count[0]
        count[0] += 1
        copy = pltpu.make_async_copy(src, dst, recv_sem.at[n])
        copy.start()
        return copy.wait

    pending = {}

    def finish(*key):
        for wait in pending.pop(key):
            wait()

    own_rows = pl.ds(pl.multiple_of(core * 8, 8), 8)
    other_rows = pl.ds(pl.multiple_of((1 - core) * 8, 8), 8)

    def slot(ref, lead, at, rows):
        at = tuple(at.get(axis, slice(None)) for axis in "zpyx")
        return ref.at[(*lead, *at) if rows is None else (*lead, *at, rows)]

    def swap(src, s_lead, dst, d_lead, axes, rows, forward):
        waits = []
        for ks in itertools.product(*(range(SIZE[axis]) for axis in axes)):
            to = {axis: around(axis, k) for axis, k in zip(axes, ks)}
            take, put = dict(to), {axis: me[axis] for axis in axes}
            if "z" in axes:
                if forward:
                    take["z"] = lax.rem(eff + ks[axes.index("z")], 2)
                else:
                    put["z"] = eff
            pair = slot(src, s_lead, take, rows), slot(dst, d_lead, put, rows)
            waits.append(remote(*pair, device(**to)) if any(ks) else local(*pair))
        return waits

    bufs = (b0, b1, b2)

    def start(a, j, c, u):
        half = core if u else 1 - core
        pending["a2a", a, j, c, u] = swap(
            bufs[a], (j, c, half), bufs[a], (j + 1, c, half), AXES[a][c][u][j], None, a != 1
        )

    wts[0] = jnp.full((8, 128), wt_ref[0], F32)
    pending["wc",] = [remote(wts.at[0], wts.at[1], device(k=1 - core))]

    def weights():
        finish("wc")
        wts[2] = wts[0] + wts[1]
        pending["wh",] = [
            remote(wts.at[2], wts.at[2 + k], device(h=lax.rem(zh + k, 4))) for k in range(1, 4)
        ]

    def total_weight():
        finish("wh")
        wts[6] = 1.0 / (wts[2] + wts[3] + (wts[4] + wts[5]))

    def step_adv(a, j, c, u):
        finish("a2a", a, j, c, u)
        start(a, j + 1, c, u)

    def step_conv(a, h):
        cols = slice(h * 256, h * 256 + 256)

        def along_y(m, carry):
            rows = pl.ds(pl.multiple_of(m * 256, 256), 256)
            x = dot(whi[rows, :], gyh[:, cols]) + (dot(wlo[rows, :], gyh[:, cols]) + dot(whi[rows, :], gyl[:, cols]))
            hi, lo = split(x)
            thi[rows, :] = hi
            tlo[rows, :] = lo
            return carry
        lax.fori_loop(0, 4, along_y, 0)

        for p in range(2):
            def along_x(m, carry):
                rows = pl.ds(pl.multiple_of(m * 128, 128), 128)
                k = slice(p * 512, p * 512 + 512)
                x = dot(gxh[rows, :], thi[k, :]) + (dot(gxl[rows, :], thi[k, :]) + dot(gxh[rows, :], tlo[k, :]))
                for e in range(2):
                    block = x[:, e * 128 : e * 128 + 128].reshape(2, 4, 2, 8, 128)
                    for half in range(2):
                        bufs[a][0, 2 * h + e, half, :, p, m] = block[:, :, half]
                return carry
            lax.fori_loop(0, 4, along_x, 0)
        for e in range(2):
            start(a, 0, 2 * h + e, 0)
            start(a, 0, 2 * h + e, 1)
        if a == 0 and h == 1:
            weights()

    def columns(x):
        hi, lo = split(x)
        return dot(gz3[...], jnp.concatenate([hi, lo, hi], axis=0))

    def convolved(a, c, half):
        flat = bufs[a].at[2, c, half].reshape(512, 128)
        weight = wt_ref[0]

        def pair(n, carry):
            r = half * 8 + n * 2
            x = jnp.concatenate([flat[pl.ds(n * 2 + e, 64, stride=8), :] for e in range(2)], axis=1)
            y = columns(x)
            for e in range(2):
                part = y[:, e * 128 : e * 128 + 128]
                if a == 0:
                    d_ref[c, r + e] = part
                else:
                    part = d_ref[c, r + e] * part
                t_ref[a // 2, c, r + e] = weight * jnp.log(part)
            return carry
        lax.fori_loop(0, 4, pair, 0)

    def step_zo(a, c):
        ph = a // 2
        finish("a2a", a, 1, c, 0)
        convolved(a, c, 1 - core)
        pending["cs", ph, c] = [remote(t_ref.at[ph, c, other_rows], cb_ref.at[ph, c], device(k=1 - core))]

    def step_zw(a, c):
        finish("a2a", a, 1, c, 1)
        convolved(a, c, core)

    mine = pl.ds(quarter * 2, 2)
    given = pl.ds(bit_one * 4 + (1 - bit_two) * 2, 2)
    half_mine = pl.ds(bit_one * 4, 4)
    half_given = pl.ds((1 - bit_one) * 4, 4)

    def step_cs(a, c):
        ph = a // 2
        finish("cs", ph, c)
        u_ref[ph, c] = t_ref[ph, c, own_rows] + cb_ref[ph, c]
        pending["rs1", ph, c] = [remote(u_ref.at[ph, c, half_given], r1_ref.at[ph, c], one)]

    def step_rs1(a, c):
        ph = a // 2
        finish("rs1", ph, c)
        u_ref[ph, c, half_mine] += r1_ref[ph, c]
        pending["rs2", ph, c] = [remote(u_ref.at[ph, c, given], r2_ref.at[ph, c], two)]

    def step_rs2(a, c):
        ph = a // 2
        if ("wh",) in pending:
            total_weight()
        finish("rs2", ph, c)
        total = u_ref[ph, c, mine] + r2_ref[ph, c]
        mean = jnp.exp(total * wts[6, 0:1, 0:1].reshape(1, 1, 1))
        if a == 0:
            bar_ref[c, mine] = mean
            here = bar_ref.at[c, mine]
            pending["ag1", c] = [remote(here, here, two)]
        else:
            flat = share_ref.at[0].reshape(512, 128)
            for e in range(2):
                flat[pl.ds(c * 2 + e, 64, stride=8), :] = mean[e]

    def step_ag1(a, c):
        finish("ag1", c)
        here = bar_ref.at[c, half_mine]
        pending["ag2", c] = [remote(here, here, one)]

    def step_ag2(a, c):
        finish("ag2", c)
        pending["cg", c] = [remote(bar_ref.at[c], oth_ref.at[c], device(k=1 - core))]

    def scaled(src, c, half):
        flat = b1.at[0, c, half].reshape(512, 128)

        def pair(n, carry):
            r = half * 8 + n * 2
            parts = []
            for e in range(2):
                v = src[c, n * 2 + e] / d_ref[c, r + e]
                d_ref[c, r + e] = v
                parts.append(v)
            y = columns(jnp.concatenate(parts, axis=1))
            for e in range(2):
                flat[pl.ds(n * 2 + e, 64, stride=8), :] = y[:, e * 128 : e * 128 + 128]
            return carry
        lax.fori_loop(0, 4, pair, 0)

    def step_zbw(a, c):
        scaled(bar_ref, c, core)
        start(1, 0, c, 1)

    def step_zbo(a, c):
        finish("cg", c)
        scaled(oth_ref, c, 1 - core)
        start(1, 0, c, 0)

    def step_xb(h):
        for e in range(2):
            finish("a2a", 1, 1, 2 * h + e, 0)
            finish("a2a", 1, 1, 2 * h + e, 1)
        cols = slice(h * 256, h * 256 + 256)
        for p in range(2):
            def block(c, k):
                halves = [b1[2, c, half, k % 2, p, k // 2][:, None] for half in range(2)]
                return jnp.concatenate(halves, axis=1).reshape(64, 128)

            x = jnp.concatenate(
                [jnp.concatenate([block(2 * h + e, k) for k in range(8)], axis=0) for e in range(2)], axis=1
            )
            hi, lo = split(x)
            thi[p * 512 : p * 512 + 512, :] = hi
            tlo[p * 512 : p * 512 + 512, :] = lo

            def along_x(m, carry):
                rows = pl.ds(pl.multiple_of(m * 128, 128), 128)
                to = pl.ds(pl.multiple_of(p * 512 + m * 128, 128), 128)
                k = slice(p * 512, p * 512 + 512)
                x = dot(gxh[rows, :], thi[k, :]) + (dot(gxl[rows, :], thi[k, :]) + dot(gxh[rows, :], tlo[k, :]))
                hi, lo = split(x)
                whi[to, cols] = hi
                wlo[to, cols] = lo
                return carry
            lax.fori_loop(0, 4, along_x, 0)

    def over_lanes(rows, cols):
        a_hi, a_lo = whi[rows, cols], wlo[rows, cols]
        return dot(a_hi, gyh[cols, :]) + (dot(a_lo, gyh[cols, :]) + dot(a_hi, gyl[cols, :]))

    def step_ya():
        def along_y(m, carry):
            rows = pl.ds(pl.multiple_of(m * 128, 128), 128)
            w_ref[rows, :] = over_lanes(rows, slice(0, 256))
            return carry
        lax.fori_loop(0, 8, along_y, 0)

    def step_yb():
        def along_y(m, carry):
            rows = pl.ds(pl.multiple_of(m * 128, 128), 128)
            w = dens_ref[rows, :] / (w_ref[rows, :] + over_lanes(rows, slice(256, 512)))
            w_ref[rows, :] = w
            hi, lo = split(w)
            whi[rows, :] = hi
            wlo[rows, :] = lo
            return carry
        lax.fori_loop(0, 8, along_y, 0)
        copy = pltpu.make_async_copy(w_ref, w_hbm, io_sem.at[1])
        copy.start()
        outs.append(copy)

    def part(ref, h):
        return ref.at[..., pl.ds(h * 4, 4), :]

    def step_tx(h):
        pending["tail", h] = swap(share_ref, (0,), share_ref, (1,), "x", pl.ds(h * 4, 4), False)

    def step_ty(h):
        finish("tail", h)
        pending["tail", h] = swap(share_ref, (1,), gath_ref, (core, zh), "yz", pl.ds(h * 4, 4), False)

    def both(to_right, to_left):
        return [remote(to_right, to_right, device(h=right)), remote(to_left, to_left, device(h=left))]

    def across(h, *at):
        here = part(gath_ref.at[(core,) + at], h)
        pending["over", h].append(remote(here, here, device(k=1 - core)))

    def step_tg(h):
        finish("tail", h)
        here = part(gath_ref.at[core, zh], h)
        pending["tail", h] = both(here, here)
        pending["over", h] = []
        across(h, zh)

    def step_th(h):
        finish("tail", h)
        pending["tail", h] = both(part(gath_ref.at[core, left, 0], h), part(gath_ref.at[core, right, 1], h))
        across(h, left)
        across(h, right)

    def step_ti(h):
        finish("tail", h)
        across(h, far)

    def step_tp(h):
        def place(k):
            for h_from in range(NHD):
                for z in range(2):
                    src = gath_ref.at[k, h_from, z].reshape(256, 128)
                    bits = h_from // 2, (h_from + h_from // 2) % 2
                    row = bits[z] * 4 + bits[1 - z] * 2
                    for c in (2 * h, 2 * h + 1):
                        dst = bary_ref.at[c, z]
                        for e in range(2):
                            dst[pl.ds(k * 8 + row + e, 32, stride=16), :] = src[pl.ds(c * 2 + e, 32, stride=8), :]

        place(core)
        finish("over", h)
        place(1 - core)
        for c in (2 * h, 2 * h + 1):
            for z in range(2):
                copy = pltpu.make_async_copy(
                    bary_ref.at[c, z].reshape(8, 64, 128), bary_hbm.at[:, z, :, pl.ds(c * 128, 128)], io_sem.at[2 + 2 * c + z]
                )
                copy.start()
                outs.append(copy)

    table = {
        "conv": step_conv, "adv": step_adv, "zo": step_zo, "zw": step_zw, "cs": step_cs, "rs1": step_rs1, "rs2": step_rs2,
        "ag1": step_ag1, "ag2": step_ag2, "zbw": step_zbw, "zbo": step_zbo, "xb": step_xb, "ya": step_ya, "yb": step_yb,
        "tx": step_tx, "ty": step_ty, "tg": step_tg, "th": step_th, "ti": step_ti, "tp": step_tp,
    }
    for name, *rest in ORDER:
        table[name](*rest)
    for copy in sent:
        copy.wait_send()
    for copy in outs:
        copy.wait()
    assert count[0] <= SEMS and not pending


SEMS = 384
LIVE = 100


def local(densities, weights, spreads):
    field = (3, CH, 2, 2, 2, 4, 4, 8, 128)
    vmem = pltpu.VMEM
    scratch = [
        vmem((1024, 512), F32), vmem((1024, 512), F32), vmem((CH, 2, 512, 128), F32), vmem((512, 128), F32),
        vmem(field, F32), vmem(field, F32), vmem(field, F32),
        vmem((CH, 16, 64, 128), F32),
        vmem((2, CH, 16, 64, 128), F32),
        vmem((2, CH, 8, 64, 128), F32),
        vmem((2, CH, 8, 64, 128), F32),
        vmem((2, CH, 4, 64, 128), F32),
        vmem((2, CH, 2, 64, 128), F32),
        vmem((CH, 8, 64, 128), F32),
        vmem((CH, 8, 64, 128), F32),
        vmem((2, 2, 2, 4, 4, 8, 128), F32),
        vmem((2, 4, 2, 2, 4, 4, 8, 128), F32),
        vmem((1024, 512), BF), vmem((1024, 512), BF),
        vmem((1024, 256), BF), vmem((1024, 256), BF),
        vmem((512, 512), BF), vmem((512, 512), BF), vmem((512, 512), BF), vmem((512, 512), BF),
        vmem((64, 192), BF),
        vmem((7, 8, 128), F32),
        pltpu.SemaphoreType.DMA((10,)), pltpu.SemaphoreType.DMA((LIVE,)), pltpu.SemaphoreType.DMA((SEMS,)),
    ]
    whole = pl.BlockSpec(memory_space=pl.ANY)
    smem = pl.BlockSpec(memory_space=pltpu.SMEM)
    bary, scale_w = pl.pallas_call(
        body,
        out_shape=[
            jax.ShapeDtypeStruct((8, 2, 64, 512), F32),
            jax.ShapeDtypeStruct((1024, 512), F32),
        ],
        in_specs=[whole, smem, smem],
        out_specs=[whole, whole],
        scratch_shapes=scratch,
        compiler_params=pltpu.CompilerParams(
            collective_id=0, has_side_effects=True, vmem_limit_bytes=61 * 1024 * 1024
        ),
        name="sinkhorn",
    )(densities.reshape(1024, 512), weights, spreads)
    return bary.reshape(2, 512, 512), scale_w.reshape(1, 2, 512, 512)


def solution(mesh):
    return jax.shard_map(
        local,
        mesh=mesh,
        in_specs=(P("dens", "sp", None, None), P("dens"), P()),
        out_specs=(P("sp", None, None), P("dens", "sp", None, None)),
        check_vma=False,
    )
```
